128 devices in a mesh: dom: 32 (over y, x, z_lo), feat: 4 (over z_hi, core).
Axes of the slice: x: 4, y: 4, z: 4 (z_hi: 2, z_lo: 2; z = z_hi * 2 + z_lo), core: 2. Of those that a mesh axis runs over, the one named last changes fastest.
Arguments:
- features: bfloat16 [65536, 256], P('dom', 'feat'), may hold values from -6 to 6
- hub_feats: bfloat16 [4096, 256], P('dom', 'feat'), may hold values from -6 to 6
- hub_coef: bfloat16 [65536, 4096], P('dom'), may hold values from 0 to 0.024291992
- tile_coef: bfloat16 [3072, 128, 128], P('dom'), may hold values from 0 to 0.024291992
- tile_index: int32 [3072, 2], P('dom'), may hold values from 0 to 79, as said below
- boundary_rows: int32 [32, 32, 256], P('dom'), may hold values from -1 to 2047, as said below
- self_weight: bfloat16 [256, 256], P('feat'), may hold values from -0.375 to 0.375
- neigh_weight: bfloat16 [256, 256], P('feat'), may hold values from -0.375 to 0.375
- out_grad: bfloat16 [65536, 256], P('dom', 'feat'), may hold values from -6 to 6
Outputs:
- output_rows: bfloat16 [65536, 256], P('dom', 'feat')
- grad_feats: float32 [65536, 256], P('dom', 'feat')
- grad_hubs: float32 [4096, 256], P('dom', 'feat')
The draws below stay inside these ranges and needn't reach their ends.
Inputs may be any that keep to these rules, and one draw needn't show every extreme that they name: `tile_index`: column 0 names a destination among the partition's 16 node tiles. Column 1 names a source tile: below 16 one of the partition's own tiles, else tile 16 + q * 2 + j is tile j of the rows received from partition q. Within each partition's 96 rows every received tile is a source exactly once. `boundary_rows`: entry [q, r, k] is a row among partition q's 2048 non-hub nodes whose features reader r needs, or -1 for an empty slot; the live entries of [q, r] come first and are distinct.
All inputs are finite; a program needn't handle non-finite values.
Results may differ from the reference program's by a relative error of at most 0.0037.
Values may be sent and summed in bfloat16 or wider, within the bound.
No kernel may reach another device: no remote copies, remote signals or barrier semaphores. Data moves between devices by JAX's collectives and lax.ppermute only.
A program may use at most 128 MiB of HBM per device.

```python
import jax
import jax.numpy as jnp
from jax import lax

D = 256
HID = 256
TILE = 128
NODE_TILES = 16
SEND_TILES = 2
NODES_DEV = 2048
NODES = 65536
HUBS = 4096
SLOTS = 256
LOCAL_TILES = 32
TILES = 96
ALL_TILES = 3072
SOURCE_TILES = 80
N_DOM = 32


def draw_tile_index(key, part):
    key = jax.random.fold_in(key, 11)
    received = NODE_TILES + jnp.arange(N_DOM * SEND_TILES, dtype=jnp.int32)

    def one_device(device_key):
        perm_key, order_key, target_key = jax.random.split(device_key, 3)
        local_tiles = (jax.random.permutation(perm_key, LOCAL_TILES).astype(jnp.int32) % NODE_TILES).astype(jnp.int32)
        sources = jnp.concatenate([received, local_tiles])
        sources = sources[jax.random.permutation(order_key, TILES)]
        targets = jax.random.randint(target_key, (TILES,), 0, NODE_TILES, dtype=jnp.int32)
        return jnp.stack([targets, sources], 1)
    return jax.vmap(one_device)(jax.random.split(key, N_DOM)).reshape(N_DOM * TILES, 2).astype(jnp.int32)


def draw_boundary_rows(key, part):
    key = jax.random.fold_in(key, 23)
    row_key, left_key, second_random_key = jax.random.split(key, 3)
    pair_keys = jax.random.split(row_key, N_DOM * N_DOM)
    chosen = jax.vmap(lambda k: jax.random.permutation(k, NODES_DEV)[:SLOTS])(pair_keys)
    chosen = chosen.reshape(N_DOM, N_DOM, SLOTS).astype(jnp.int32)
    left_draw = jax.random.randint(left_key, (N_DOM, N_DOM), 0, SLOTS, dtype=jnp.int32)
    right_draw = jax.random.randint(second_random_key, (N_DOM, N_DOM), 0, SLOTS, dtype=jnp.int32)
    counts = SLOTS - left_draw * right_draw // SLOTS
    sender = jnp.arange(N_DOM, dtype=jnp.int32)[:, None]
    reader = jnp.arange(N_DOM, dtype=jnp.int32)[None, :]
    counts = jnp.where(reader == (sender + 1) % N_DOM, SLOTS, counts)
    slot_pos = jnp.arange(SLOTS, dtype=jnp.int32)
    return jnp.where(slot_pos[None, None, :] < counts[:, :, None], chosen, -1).astype(jnp.int32)


def block_levels(key, extent, cuts, smallest, top_value):
    loudness, own = 1.0, jax.random.fold_in(key, 6)
    for axis_at, parts in cuts:
        draws = jnp.exp(jax.random.uniform(jax.random.fold_in(own, axis_at), (parts,), jnp.float32, smallest / len(cuts), top_value / len(cuts)))
        loudness = loudness * jnp.repeat(draws, extent[axis_at] // parts).reshape([-1 if axis == axis_at else 1 for axis in range(len(extent))])
    return loudness


def scatter_about(stream_key, dims, spread, most, pieces=(), kind=jnp.bfloat16):
    drawn = jax.random.normal(stream_key, dims, jnp.float32) * spread
    if len(pieces) > 0:
        drawn = block_levels(stream_key, dims, pieces, -0.22, 0.18) * drawn
    return jnp.clip(drawn, min=-most, max=most).astype(kind)


def setup_inputs(seed: int = 0) -> dict:
    seeds = jax.random.split(jax.random.key(seed), 10)
    return {
        "features": scatter_about(seeds[0], (NODES, D), 1.0, 6.0, ((0, 32), (1, 4))),
        "hub_feats": scatter_about(seeds[1], (HUBS, D), 1.0, 6.0, ((0, 32), (1, 4))),
        "hub_coef": jnp.clip(0.024291992 * jax.random.uniform(seeds[2], (NODES, HUBS), jnp.float32) ** block_levels(seeds[2], (NODES, HUBS), ((0, 32),), -0.2, 0.2), 0.0, 0.024291992).astype(jnp.bfloat16),
        "tile_coef": jnp.clip(0.024291992 * jax.random.uniform(seeds[3], (ALL_TILES, TILE, TILE), jnp.float32) ** block_levels(seeds[3], (ALL_TILES, TILE, TILE), ((0, 32),), -0.2, 0.2), 0.0, 0.024291992).astype(jnp.bfloat16),
        "tile_index": draw_tile_index(jax.random.fold_in(seeds[9], 71), 0),
        "boundary_rows": draw_boundary_rows(jax.random.fold_in(seeds[9], 71), 0),
        "self_weight": scatter_about(seeds[6], (D, HID), D ** -0.5, 0.375, ((0, 4),)),
        "neigh_weight": scatter_about(seeds[7], (D, HID), D ** -0.5, 0.375, ((0, 4),)),
        "out_grad": scatter_about(seeds[8], (NODES, HID), 1.0, 6.0, ((0, 32), (1, 4))),
    }


def reference(features, hub_feats, hub_coef, tile_coef, tile_index, boundary_rows, self_weight, neigh_weight, out_grad):
    part_feats = features.reshape(N_DOM, NODES_DEV, D)

    def pick_rows(owner_rows, wanted):
        taken = jnp.take(owner_rows, jnp.maximum(wanted, 0), axis=0)
        return jnp.where(wanted[..., None] >= 0, taken, jnp.zeros((), owner_rows.dtype))

    sent_rows = jax.vmap(pick_rows)(part_feats, boundary_rows)
    received = jnp.swapaxes(sent_rows, 0, 1)
    part_coef = tile_coef.reshape(N_DOM, TILES, TILE, TILE)
    part_index = tile_index.reshape(N_DOM, TILES, 2)

    def forward_tiles(operands):
        own_rows, got_rows, coef_tiles, index_rows = operands
        source_every_node = jnp.concatenate([own_rows, got_rows.reshape(-1, D)], 0).reshape(SOURCE_TILES, TILE, D)
        picked = jnp.take(source_every_node, index_rows[:, 1], axis=0).astype(jnp.float32)
        partial_products = jnp.einsum('tab,tbd->tad', coef_tiles.astype(jnp.float32), picked)
        summed = jax.ops.segment_sum(partial_products, index_rows[:, 0], num_segments=NODE_TILES)
        return summed.reshape(NODES_DEV, D)

    tile_sum = lax.map(forward_tiles, (part_feats, received, part_coef, part_index)).reshape(NODES, D)
    hub_total_sum = jnp.dot(hub_coef, hub_feats, preferred_element_type=jnp.float32)
    aggregate = (tile_sum + hub_total_sum).astype(jnp.bfloat16)
    pre_act = jnp.dot(features, self_weight, preferred_element_type=jnp.float32) + jnp.dot(aggregate, neigh_weight, preferred_element_type=jnp.float32)
    output_rows = jax.nn.elu(pre_act).astype(jnp.bfloat16)
    slope = jnp.where(pre_act > 0, jnp.ones_like(pre_act), jnp.exp(jnp.minimum(pre_act, jnp.zeros_like(pre_act))))
    grad_pre = (out_grad.astype(jnp.float32) * slope).astype(jnp.bfloat16)
    self_back = jnp.dot(grad_pre, self_weight.T, preferred_element_type=jnp.float32)
    grad_agg = jnp.dot(grad_pre, neigh_weight.T, preferred_element_type=jnp.float32).astype(jnp.bfloat16)
    grad_hubs = jnp.dot(hub_coef.T, grad_agg, preferred_element_type=jnp.float32)

    def backward_tiles(operands):
        grad_rows, coef_tiles, index_rows = operands
        target_rows = jnp.take(grad_rows.reshape(NODE_TILES, TILE, D), index_rows[:, 0], axis=0).astype(jnp.float32)
        terms = jnp.einsum('tab,tad->tbd', coef_tiles.astype(jnp.float32), target_rows)
        source_grad = jax.ops.segment_sum(terms, index_rows[:, 1], num_segments=SOURCE_TILES).reshape(-1, D)
        return source_grad[:NODES_DEV], source_grad[NODES_DEV:].reshape(N_DOM, SLOTS, D)

    own_grad, back_grad = lax.map(backward_tiles, (grad_agg.reshape(N_DOM, NODES_DEV, D), part_coef, part_index))
    offsets = (jnp.arange(N_DOM, dtype=jnp.int32) * NODES_DEV)[:, None, None]
    flat_index = jnp.where(boundary_rows >= 0, boundary_rows + offsets, NODES).astype(jnp.int32)
    values = jnp.swapaxes(back_grad, 0, 1).reshape(-1, D)
    returned = jnp.zeros((NODES + 1, D), jnp.float32).at[flat_index.reshape(-1)].add(values)[:NODES]
    grad_feats = self_back + own_grad.reshape(NODES, D) + returned
    return (output_rows, grad_feats, grad_hubs)
```

```python
import functools

import jax
import jax.numpy as jnp
from jax import lax
from jax.experimental import pallas as pl
from jax.experimental.pallas import tpu as pltpu
from jax.sharding import PartitionSpec as P

BF = jnp.bfloat16
F32 = jnp.float32
NT = (((1,), (1,)), ((), ()))
NN = (((1,), (0,)), ((), ()))
TN = (((0,), (0,)), ((), ()))

COLS = 64
NODES = 2048
DOM = 32
FEAT = 4
SLOTS = 256
TILE = 128
TILES = 96
OWN_TILES = NODES // TILE
RECV_TILES = DOM * SLOTS // TILE
QUARTER = NODES // FEAT
LOW = 256
HIGH = NODES // LOW
HUBS = 4096

VMEM = pl.BlockSpec(memory_space=pltpu.VMEM)
SMEM = pl.BlockSpec(memory_space=pltpu.SMEM)


def dot(a, b, dims):
    return lax.dot_general(a, b, dims, preferred_element_type=F32)


def params(mib=40):
    return pltpu.CompilerParams(vmem_limit_bytes=mib * 1024 * 1024)


def one_hot(low):
    rows = lax.broadcasted_iota(jnp.int32, (LOW, low.shape[1]), 0)
    return jnp.where(rows == low, 1.0, 0.0).astype(BF)


def gather_kernel(x_ref, slot_ref, out_ref, stacked):
    for b in range(HIGH):
        stacked[b * COLS : (b + 1) * COLS, :] = x_ref[:, b * LOW : (b + 1) * LOW]

    @pl.loop(0, DOM, unroll=2)
    def _(r):
        index = slot_ref[pl.ds(r, 1), :]
        high = index >> 8
        found = dot(stacked[...], one_hot(index & (LOW - 1)), NN)
        out = jnp.zeros((COLS, SLOTS), F32)
        for b in range(HIGH):
            out = jnp.where(high == b, found[b * COLS : (b + 1) * COLS], out)
        out = out.astype(BF)
        out_ref[2 * r] = out[:, :TILE]
        out_ref[2 * r + 1] = out[:, TILE:]


def gather_rows(x, slots):
    return pl.pallas_call(
        gather_kernel,
        out_shape=jax.ShapeDtypeStruct((RECV_TILES, COLS, TILE), BF),
        in_specs=[VMEM, VMEM],
        out_specs=VMEM,
        scratch_shapes=[pltpu.VMEM((HIGH * COLS, LOW), BF)],
        compiler_params=params(),
        cost_estimate=pl.CostEstimate(flops=4 * 10**9, bytes_accessed=2**21, transcendentals=0),
        name="gather_rows",
    )(x, slots)


def hub_forward_kernel(h_ref, coef_ref, out_ref, hubs):
    @pl.when(pl.program_id(0) == 0)
    def _():
        for q in range(DOM):
            hubs[:, q * TILE : (q + 1) * TILE] = h_ref[q]

    out_ref[...] = dot(hubs[...], coef_ref[...], NT)


def hub_forward(hubs, coef):
    step = 256
    return pl.pallas_call(
        hub_forward_kernel,
        grid=(NODES // step,),
        out_shape=jax.ShapeDtypeStruct((COLS, NODES), F32),
        in_specs=[
            pl.BlockSpec((DOM, COLS, TILE), lambda i: (0, 0, 0)),
            pl.BlockSpec((step, HUBS), lambda i: (i, 0)),
        ],
        out_specs=pl.BlockSpec((COLS, step), lambda i: (0, i)),
        scratch_shapes=[pltpu.VMEM((COLS, HUBS), BF)],
        compiler_params=params(),
        cost_estimate=pl.CostEstimate(flops=2 * 10**9, bytes_accessed=2**24, transcendentals=0),
        name="hub_forward",
    )(hubs, coef)


def tile_forward_kernel(index_ref, x_ref, recv_ref, coef_ref, hub_ref, out_ref, source, total):
    for t in range(OWN_TILES):
        source[t] = x_ref[:, t * TILE : (t + 1) * TILE]
        total[t] = hub_ref[:, t * TILE : (t + 1) * TILE]
    source[OWN_TILES:] = recv_ref[...]
    group = 8

    @pl.loop(0, TILES // group)
    def _(g):
        products = []
        for k in range(group):
            c = g * group + k
            products.append(dot(source[index_ref[1, c]], coef_ref[c], NT))
        for k in range(group):
            d = index_ref[0, g * group + k]
            total[d] = total[d] + products[k]

    for t in range(OWN_TILES):
        n = t * TILE % QUARTER
        out_ref[t * TILE // QUARTER, :, n : n + TILE] = total[t].astype(BF)


def tile_forward(index, x, recv, coef, hub):
    return pl.pallas_call(
        tile_forward_kernel,
        out_shape=jax.ShapeDtypeStruct((FEAT, COLS, QUARTER), BF),
        in_specs=[SMEM, VMEM, VMEM, VMEM, VMEM],
        out_specs=VMEM,
        scratch_shapes=[
            pltpu.VMEM((OWN_TILES + RECV_TILES, COLS, TILE), BF),
            pltpu.VMEM((OWN_TILES, COLS, TILE), F32),
        ],
        compiler_params=params(),
        cost_estimate=pl.CostEstimate(flops=10**9, bytes_accessed=2**22, transcendentals=0),
        name="tile_forward",
    )(index, x, recv, coef, hub)


def dense_kernel(agg_ref, early_ref, grad_agg_ref, late_ref):
    def whole(ref, first, lanes=slice(None)):
        return jnp.concatenate([ref[f, first : first + COLS, lanes] for f in range(FEAT)], 0)

    hid = FEAT * COLS
    self_weight = whole(early_ref, 2 * COLS, slice(0, hid))
    neigh_weight = whole(early_ref, 2 * COLS, slice(hid, 2 * hid))
    pre_act = dot(self_weight, whole(early_ref, 0), TN) + dot(neigh_weight, whole(agg_ref, 0), TN)
    down = jnp.exp(jnp.minimum(pre_act, 0.0))
    output = jnp.where(pre_act > 0, pre_act, down - 1.0).astype(BF)
    slope = jnp.where(pre_act > 0, 1.0, down)
    grad_pre = (whole(early_ref, COLS).astype(F32) * slope).astype(BF)
    grad_agg = dot(neigh_weight, grad_pre, NN).astype(BF)
    self_back = dot(self_weight, grad_pre, NN).astype(BF)
    for f in range(FEAT):
        grad_agg_ref[f] = grad_agg[f * COLS : (f + 1) * COLS]
        late_ref[f, :COLS] = output[f * COLS : (f + 1) * COLS]
        late_ref[f, COLS:] = self_back[f * COLS : (f + 1) * COLS]


def dense(agg, early):
    return pl.pallas_call(
        dense_kernel,
        out_shape=(
            jax.ShapeDtypeStruct((FEAT, COLS, QUARTER), BF),
            jax.ShapeDtypeStruct((FEAT, 2 * COLS, QUARTER), BF),
        ),
        in_specs=[VMEM, VMEM],
        out_specs=(VMEM, VMEM),
        compiler_params=params(),
        cost_estimate=pl.CostEstimate(flops=10**9, bytes_accessed=2**21, transcendentals=2**17),
        name="dense",
    )(agg, early)


def tile_backward_kernel(index_ref, grad_ref, coef_ref, recv_ref, own_ref, grads, total):
    for t in range(OWN_TILES):
        n = t * TILE % QUARTER
        grads[t] = grad_ref[t * TILE // QUARTER, :, n : n + TILE]
    total[:OWN_TILES] = jnp.zeros((OWN_TILES, COLS, TILE), F32)
    total[OWN_TILES:] = jnp.zeros((RECV_TILES, COLS, TILE), F32)
    group = 8

    @pl.loop(0, TILES // group)
    def _(g):
        products = []
        for k in range(group):
            c = g * group + k
            products.append(dot(grads[index_ref[0, c]], coef_ref[c], NN))
        for k in range(group):
            s = index_ref[1, g * group + k]
            total[s] = total[s] + products[k]

    recv_ref[...] = total[OWN_TILES:].astype(BF)
    for t in range(OWN_TILES):
        own_ref[:, t * TILE : (t + 1) * TILE] = total[t]


def tile_backward(index, grad, coef):
    return pl.pallas_call(
        tile_backward_kernel,
        out_shape=(
            jax.ShapeDtypeStruct((RECV_TILES, COLS, TILE), BF),
            jax.ShapeDtypeStruct((COLS, NODES), F32),
        ),
        in_specs=[SMEM, VMEM, VMEM],
        out_specs=(VMEM, VMEM),
        scratch_shapes=[
            pltpu.VMEM((OWN_TILES, COLS, TILE), BF),
            pltpu.VMEM((OWN_TILES + RECV_TILES, COLS, TILE), F32),
        ],
        compiler_params=params(),
        cost_estimate=pl.CostEstimate(flops=10**9, bytes_accessed=2**22, transcendentals=0),
        name="tile_backward",
    )(index, grad, coef)


def hub_backward_kernel(grad_ref, coef_ref, out_ref, grads):
    @pl.when(pl.program_id(0) == 0)
    def _():
        for f in range(FEAT):
            grads[:, f * QUARTER : (f + 1) * QUARTER] = grad_ref[f]

    terms = dot(grads[...], coef_ref[...], NN).astype(BF)
    for k in range(out_ref.shape[0]):
        out_ref[k] = terms[:, k * TILE : (k + 1) * TILE]


def hub_backward(grad, coef):
    step = 512
    return pl.pallas_call(
        hub_backward_kernel,
        grid=(HUBS // step,),
        out_shape=jax.ShapeDtypeStruct((DOM, COLS, TILE), BF),
        in_specs=[
            pl.BlockSpec((FEAT, COLS, QUARTER), lambda i: (0, 0, 0)),
            pl.BlockSpec((NODES, step), lambda i: (0, i)),
        ],
        out_specs=pl.BlockSpec((step // TILE, COLS, TILE), lambda i: (i, 0, 0)),
        scratch_shapes=[pltpu.VMEM((COLS, NODES), BF)],
        compiler_params=params(),
        cost_estimate=pl.CostEstimate(flops=2 * 10**9, bytes_accessed=2**24, transcendentals=0),
        name="hub_backward",
    )(grad, coef)


def scatter_kernel(slot_ref, recv_ref, own_ref, late_ref, out_ref, total):
    total[...] = jnp.zeros_like(total)
    group = 4

    @pl.loop(0, DOM // group)
    def _(g):
        spread, hots = [], []
        for k in range(group):
            r = g * group + k
            index = slot_ref[pl.ds(r, 1), :]
            high = index >> 8
            rows = jnp.concatenate([recv_ref[2 * r], recv_ref[2 * r + 1]], 1)
            spread.append(
                jnp.concatenate([jnp.where(high == b, rows, jnp.zeros_like(rows)) for b in range(HIGH)], 0)
            )
            hots.append(one_hot(index & (LOW - 1)))
        total[...] += dot(jnp.concatenate(spread, 1), jnp.concatenate(hots, 1), NT)

    for b in range(HIGH):
        lanes = slice(b * LOW, (b + 1) * LOW)
        n = b * LOW % QUARTER
        back = late_ref[b * LOW // QUARTER, COLS:, n : n + LOW].astype(F32)
        out_ref[:, lanes] = total[b * COLS : (b + 1) * COLS] + own_ref[:, lanes] + back


def scatter_rows(slots, recv, own, late):
    return pl.pallas_call(
        scatter_kernel,
        out_shape=jax.ShapeDtypeStruct((COLS, NODES), F32),
        in_specs=[VMEM, VMEM, VMEM, VMEM],
        out_specs=VMEM,
        scratch_shapes=[pltpu.VMEM((HIGH * COLS, LOW), F32)],
        compiler_params=params(),
        cost_estimate=pl.CostEstimate(flops=4 * 10**9, bytes_accessed=2**21, transcendentals=0),
        name="scatter_rows",
    )(slots, recv, own, late)


def quarters(x):
    return jnp.swapaxes(x.reshape(COLS, FEAT, QUARTER), 0, 1)


def body(
    features,
    hub_feats,
    hub_coef,
    tile_coef,
    tile_index,
    boundary_rows,
    self_weight,
    neigh_weight,
    out_grad,
):
    x = features.T
    slots = boundary_rows[0]
    index = tile_index.T
    to_dom = functools.partial(lax.all_to_all, axis_name="dom", split_axis=0, concat_axis=0, tiled=True)
    to_feat = functools.partial(lax.all_to_all, axis_name="feat", split_axis=0, concat_axis=0, tiled=True)

    hubs = to_dom(jnp.broadcast_to(hub_feats.T[None], (DOM, COLS, TILE)))
    outgoing = gather_rows(x, slots)
    incoming = to_dom(outgoing)

    weights = jnp.concatenate([self_weight, neigh_weight], 1)
    early = to_feat(
        jnp.concatenate(
            [quarters(x), quarters(out_grad.T), jnp.broadcast_to(weights[None], (FEAT, COLS, QUARTER))], 1
        )
    )
    hub_part = hub_forward(hubs, hub_coef)
    aggregate = tile_forward(index, x, incoming, tile_coef, hub_part)
    grad_quarter, late_quarter = dense(to_feat(aggregate), early)
    grad_agg = to_feat(grad_quarter)
    halo_back, own_grad = tile_backward(index, grad_agg, tile_coef)
    returned = to_dom(halo_back)
    hub_terms = hub_backward(grad_agg, hub_coef)
    late = to_feat(late_quarter)
    hub_arrived = to_dom(hub_terms)
    grad_feats = scatter_rows(slots, returned, own_grad, late)
    grad_hubs = jnp.sum(hub_arrived.astype(F32), 0)
    output_rows = jnp.swapaxes(late[:, :COLS], 0, 1).reshape(COLS, NODES)
    return (output_rows.T, grad_feats.T, grad_hubs.T)


def solution(mesh):
    return jax.shard_map(
        body,
        mesh=mesh,
        in_specs=(
            P("dom", "feat"),
            P("dom", "feat"),
            P("dom", None),
            P("dom", None, None),
            P("dom", None),
            P("dom", None, None),
            P("feat", None),
            P("feat", None),
            P("dom", "feat"),
        ),
        out_specs=(P("dom", "feat"), P("dom", "feat"), P("dom", "feat")),
        check_vma=False,
    )
```

```python
import jax
import jax.numpy as jnp
from jax import lax
from jax.experimental import pallas as pl
from jax.experimental.pallas import tpu as pltpu
from jax.sharding import PartitionSpec as P

BF = jnp.bfloat16
F32 = jnp.float32
NT = (((1,), (1,)), ((), ()))
NN = (((1,), (0,)), ((), ()))
TN = (((0,), (0,)), ((), ()))

COLS = 64
NODES = 2048
DOM = 32
FEAT = 4
SLOTS = 256
TILE = 128
TILES = 96
OWN_TILES = NODES // TILE
RECV_TILES = DOM * SLOTS // TILE
QUARTER = NODES // FEAT
LOW = 256
HIGH = NODES // LOW
HUBS = 4096

VMEM = pl.BlockSpec(memory_space=pltpu.VMEM)
SMEM = pl.BlockSpec(memory_space=pltpu.SMEM)


def dot(a, b, dims):
    return lax.dot_general(a, b, dims, preferred_element_type=F32)


def params(mib=40):
    return pltpu.CompilerParams(vmem_limit_bytes=mib * 1024 * 1024)


def one_hot(low):
    rows = lax.broadcasted_iota(jnp.int32, (LOW, low.shape[1]), 0)
    return jnp.where(rows == low, 1.0, 0.0).astype(BF)


def gather_kernel(x_ref, slot_ref, hub_ref, out_ref, stacked):
    for b in range(HIGH):
        stacked[b * COLS : (b + 1) * COLS, :] = x_ref[:, b * LOW : (b + 1) * LOW]

    @pl.loop(0, DOM, unroll=4)
    def _(r):
        index = slot_ref[pl.ds(r, 1), :]
        high = index >> 8
        found = dot(stacked[...], one_hot(index & (LOW - 1)), NN)
        out = jnp.zeros((COLS, SLOTS), F32)
        for b in range(HIGH):
            out = jnp.where(high == b, found[b * COLS : (b + 1) * COLS], out)
        out = out.astype(BF)
        out_ref[r, 0] = out[:, :TILE]
        out_ref[r, 1] = out[:, TILE:]
        out_ref[r, 2] = hub_ref[...]


def gather_rows(x, slots, hubs):
    return pl.pallas_call(
        gather_kernel,
        out_shape=jax.ShapeDtypeStruct((DOM, 3, COLS, TILE), BF),
        in_specs=[VMEM, VMEM, VMEM],
        out_specs=VMEM,
        scratch_shapes=[pltpu.VMEM((HIGH * COLS, LOW), BF)],
        compiler_params=params(),
        cost_estimate=pl.CostEstimate(flops=4 * 10**9, bytes_accessed=2**21, transcendentals=0),
        name="gather_rows",
    )(x, slots, hubs)


def forward_kernel(feat_ref, index_ref, x_ref, recv_ref, tile_ref, hub_ref, *rest):
    outs, (source, hubs, total) = rest[:FEAT], rest[FEAT:]
    step = pl.program_id(0)
    steps = pl.num_programs(0)
    step_tiles = OWN_TILES // 8
    group = TILES // 8

    @pl.when(step == 0)
    def _():
        for t in range(OWN_TILES):
            source[t] = x_ref[:, t * TILE : (t + 1) * TILE]
        for q in range(DOM):
            source[OWN_TILES + 2 * q] = recv_ref[q, 0]
            source[OWN_TILES + 2 * q + 1] = recv_ref[q, 1]
            hubs[:, q * TILE : (q + 1) * TILE] = recv_ref[q, 2]
        total[...] = jnp.zeros_like(total)

    products = []
    for k in range(group):
        c = step * group + k
        products.append(dot(tile_ref[c], source[index_ref[1, c]], NT))
    hub_part = dot(hub_ref[...], hubs[...], NT)
    for k in range(group):
        d = index_ref[0, step * group + k]
        total[d] = total[d] + products[k]
    for k in range(step_tiles):
        t = step * step_tiles + k
        total[t] = total[t] + hub_part[k * TILE : (k + 1) * TILE]

    @pl.when(step == steps - 1)
    def _():
        for k in range(FEAT):
            first = (feat_ref[0] ^ k) * (QUARTER // TILE)
            for j in range(QUARTER // TILE):
                outs[k][:, j * TILE : (j + 1) * TILE] = total[first + j].T.astype(BF)


def forward(feat, index, x, recv, tiles, hub_coef):
    whole = lambda shape: pl.BlockSpec(shape, lambda i: (0,) * len(shape))
    step = NODES // 8
    return pl.pallas_call(
        forward_kernel,
        grid=(8,),
        out_shape=[jax.ShapeDtypeStruct((COLS, QUARTER), BF)] * FEAT,
        in_specs=[
            SMEM,
            SMEM,
            whole((COLS, NODES)),
            whole((DOM, 3, COLS, TILE)),
            whole((TILES, TILE, TILE)),
            pl.BlockSpec((step, HUBS), lambda i: (i, 0)),
        ],
        out_specs=[whole((COLS, QUARTER))] * FEAT,
        scratch_shapes=[
            pltpu.VMEM((OWN_TILES + RECV_TILES, COLS, TILE), BF),
            pltpu.VMEM((COLS, HUBS), BF),
            pltpu.VMEM((OWN_TILES, TILE, COLS), F32),
        ],
        compiler_params=params(),
        cost_estimate=pl.CostEstimate(flops=3 * 10**9, bytes_accessed=2**24, transcendentals=0),
        name="forward",
    )(feat, index, x, recv, tiles, hub_coef)


def dense_kernel(feat_ref, *rest):
    aggs, earlies, grad_outs, lates, scratch = rest[:4], rest[4:8], rest[8:12], rest[12:16], rest[16:]
    agg, x, up, weights, down_grad, output, back = scratch
    feat = feat_ref[0]
    hid = FEAT * COLS

    def rows(k):
        return pl.ds(pl.multiple_of((feat ^ k) * COLS, COLS), COLS)

    for k in range(FEAT):
        agg[rows(k)] = aggs[k][...]
        x[rows(k)] = earlies[k][:COLS]
        up[rows(k)] = earlies[k][COLS : 2 * COLS]
        weights[rows(k)] = earlies[k][2 * COLS :]
    self_weight = weights[:, :hid]
    neigh_weight = weights[:, hid:]
    pre_act = dot(self_weight, x[...], TN) + dot(neigh_weight, agg[...], TN)
    fall = jnp.exp(jnp.minimum(pre_act, 0.0))
    output[...] = jnp.where(pre_act > 0, pre_act, fall - 1.0).astype(BF)
    slope = jnp.where(pre_act > 0, 1.0, fall)
    grad_pre = (up[...].astype(F32) * slope).astype(BF)
    down_grad[...] = dot(neigh_weight, grad_pre, NN).astype(BF)
    back[...] = dot(self_weight, grad_pre, NN).astype(BF)
    for k in range(FEAT):
        grad_outs[k][...] = down_grad[rows(k)]
        lates[k][:COLS] = output[rows(k)]
        lates[k][COLS:] = back[rows(k)]


def dense(feat, aggs, earlies):
    block = pltpu.VMEM((FEAT * COLS, QUARTER), BF)
    outs = pl.pallas_call(
        dense_kernel,
        out_shape=[jax.ShapeDtypeStruct((COLS, QUARTER), BF)] * FEAT
        + [jax.ShapeDtypeStruct((2 * COLS, QUARTER), BF)] * FEAT,
        in_specs=[SMEM] + [VMEM] * 8,
        out_specs=[VMEM] * 8,
        scratch_shapes=[block] * 7,
        compiler_params=params(),
        cost_estimate=pl.CostEstimate(flops=10**9, bytes_accessed=2**21, transcendentals=2**17),
        name="dense",
    )(feat, *aggs, *earlies)
    return outs[:4], outs[4:]


def tile_backward_kernel(feat_ref, index_ref, *rest):
    grad_refs, (coef_ref, recv_ref, own_ref, grads, total) = rest[:4], rest[4:]
    for k in range(FEAT):
        first = (feat_ref[0] ^ k) * (QUARTER // TILE)
        for j in range(QUARTER // TILE):
            grads[first + j] = grad_refs[k][:, j * TILE : (j + 1) * TILE]
    total[:OWN_TILES] = jnp.zeros((OWN_TILES, COLS, TILE), F32)
    total[OWN_TILES:] = jnp.zeros((RECV_TILES, COLS, TILE), F32)
    group = 8

    @pl.loop(0, TILES // group)
    def _(g):
        products = []
        for k in range(group):
            c = g * group + k
            products.append(dot(grads[index_ref[0, c]], coef_ref[c], NN))
        for k in range(group):
            s = index_ref[1, g * group + k]
            total[s] = total[s] + products[k]

    recv_ref[...] = total[OWN_TILES:].astype(BF)
    for t in range(OWN_TILES):
        own_ref[:, t * TILE : (t + 1) * TILE] = total[t]


def tile_backward(feat, index, grad, coef):
    return pl.pallas_call(
        tile_backward_kernel,
        out_shape=(
            jax.ShapeDtypeStruct((RECV_TILES, COLS, TILE), BF),
            jax.ShapeDtypeStruct((COLS, NODES), F32),
        ),
        in_specs=[SMEM, SMEM] + [VMEM] * 5,
        out_specs=(VMEM, VMEM),
        scratch_shapes=[
            pltpu.VMEM((OWN_TILES, COLS, TILE), BF),
            pltpu.VMEM((OWN_TILES + RECV_TILES, COLS, TILE), F32),
        ],
        compiler_params=params(),
        cost_estimate=pl.CostEstimate(flops=10**9, bytes_accessed=2**22, transcendentals=0),
        name="tile_backward",
    )(feat, index, *grad, coef)


def hub_backward_kernel(feat_ref, *rest):
    grad_refs, (coef_ref, recv_ref, out_ref, grads) = rest[:4], rest[4:]

    @pl.when(pl.program_id(0) == 0)
    def _():
        for k in range(FEAT):
            grads[:, pl.ds(pl.multiple_of((feat_ref[0] ^ k) * QUARTER, QUARTER), QUARTER)] = grad_refs[k][...]

    terms = dot(grads[...], coef_ref[...], NN).astype(BF)
    for k in range(out_ref.shape[0]):
        out_ref[k, 0] = recv_ref[2 * k]
        out_ref[k, 1] = recv_ref[2 * k + 1]
        out_ref[k, 2] = terms[:, k * TILE : (k + 1) * TILE]


def hub_backward(feat, grad, coef, recv):
    step = 512
    doms = step // TILE
    piece = pl.BlockSpec((COLS, QUARTER), lambda i: (0, 0))
    return pl.pallas_call(
        hub_backward_kernel,
        grid=(HUBS // step,),
        out_shape=jax.ShapeDtypeStruct((DOM, 3, COLS, TILE), BF),
        in_specs=[SMEM]
        + [piece] * 4
        + [pl.BlockSpec((NODES, step), lambda i: (0, i)), pl.BlockSpec((2 * doms, COLS, TILE), lambda i: (i, 0, 0))],
        out_specs=pl.BlockSpec((doms, 3, COLS, TILE), lambda i: (i, 0, 0, 0)),
        scratch_shapes=[pltpu.VMEM((COLS, NODES), BF)],
        compiler_params=params(),
        cost_estimate=pl.CostEstimate(flops=2 * 10**9, bytes_accessed=2**24, transcendentals=0),
        name="hub_backward",
    )(feat, *grad, coef, recv)


def scatter_kernel(feat_ref, slot_ref, recv_ref, own_ref, *rest):
    lates, (grad_ref, hub_ref, output_ref, total) = rest[:4], rest[4:]
    total[...] = jnp.zeros_like(total)
    group = 4

    @pl.loop(0, DOM // group)
    def _(g):
        spread, hots = [], []
        for k in range(group):
            r = g * group + k
            index = slot_ref[pl.ds(r, 1), :]
            high = index >> 8
            rows = jnp.concatenate([recv_ref[r, 0], recv_ref[r, 1]], 1)
            spread.append(
                jnp.concatenate([jnp.where(high == b, rows, jnp.zeros_like(rows)) for b in range(HIGH)], 0)
            )
            hots.append(one_hot(index & (LOW - 1)))
        total[...] += dot(jnp.concatenate(spread, 1), jnp.concatenate(hots, 1), NT)

    hub = jnp.zeros((COLS, TILE), F32)
    for r in range(DOM):
        hub = hub + recv_ref[r, 2].astype(F32)
    hub_ref[...] = hub
    for b in range(HIGH):
        lanes = slice(b * LOW, (b + 1) * LOW)
        grad_ref[:, lanes] = total[b * COLS : (b + 1) * COLS] + own_ref[:, lanes]
    for k in range(FEAT):
        lanes = pl.ds(pl.multiple_of((feat_ref[0] ^ k) * QUARTER, QUARTER), QUARTER)
        grad_ref[:, lanes] = grad_ref[:, lanes] + lates[k][COLS:].astype(F32)
        output_ref[:, lanes] = lates[k][:COLS]


def scatter_rows(feat, slots, recv, own, late):
    return pl.pallas_call(
        scatter_kernel,
        out_shape=(
            jax.ShapeDtypeStruct((COLS, NODES), F32),
            jax.ShapeDtypeStruct((COLS, TILE), F32),
            jax.ShapeDtypeStruct((COLS, NODES), BF),
        ),
        in_specs=[SMEM] + [VMEM] * 7,
        out_specs=(VMEM, VMEM, VMEM),
        scratch_shapes=[pltpu.VMEM((HIGH * COLS, LOW), F32)],
        compiler_params=params(),
        cost_estimate=pl.CostEstimate(flops=4 * 10**9, bytes_accessed=2**21, transcendentals=0),
        name="scatter_rows",
    )(feat, slots, recv, own, *late)


def to_dom(x):
    return lax.all_to_all(x, "dom", split_axis=0, concat_axis=0, tiled=True)


def to_feat(parts):
    return [parts[0]] + [
        lax.ppermute(parts[k], "feat", [(f, f ^ k) for f in range(FEAT)]) for k in range(1, FEAT)
    ]


def body(
    features,
    hub_feats,
    hub_coef,
    tile_coef,
    tile_index,
    boundary_rows,
    self_weight,
    neigh_weight,
    out_grad,
):
    x = features.T
    up = out_grad.T
    slots = boundary_rows[0]
    index = tile_index.T
    feat = lax.axis_index("feat")
    feat_ref = feat.reshape(1)
    weights = jnp.concatenate([self_weight, neigh_weight], 1)

    def early_part(k):
        first = (feat ^ k) * QUARTER
        return jnp.concatenate(
            [
                lax.dynamic_slice_in_dim(x, first, QUARTER, 1),
                lax.dynamic_slice_in_dim(up, first, QUARTER, 1),
                weights,
            ],
            0,
        )

    incoming = to_dom(gather_rows(x, slots, hub_feats.T))
    early = to_feat([early_part(k) for k in range(FEAT)])
    aggregate = forward(feat_ref, index, x, incoming, tile_coef, hub_coef)
    grad_parts, late_parts = dense(feat_ref, to_feat(aggregate), early)
    grad_agg = to_feat(grad_parts)
    halo_back, own_grad = tile_backward(feat_ref, index, grad_agg, tile_coef)
    returned = to_dom(hub_backward(feat_ref, grad_agg, hub_coef, halo_back))
    late = to_feat(late_parts)
    grad_feats, grad_hubs, output_rows = scatter_rows(feat_ref, slots, returned, own_grad, late)
    return (output_rows.T, grad_feats.T, grad_hubs.T)


def solution(mesh):
    return jax.shard_map(
        body,
        mesh=mesh,
        in_specs=(
            P("dom", "feat"),
            P("dom", "feat"),
            P("dom", None),
            P("dom", None, None),
            P("dom", None),
            P("dom", None, None),
            P("feat", None),
            P("feat", None),
            P("dom", "feat"),
        ),
        out_specs=(P("dom", "feat"), P("dom", "feat"), P("dom", "feat")),
        check_vma=False,
    )
```

```python
import jax
import jax.numpy as jnp
from jax import lax
from jax.experimental import pallas as pl
from jax.experimental.pallas import tpu as pltpu
from jax.sharding import PartitionSpec as P

BF = jnp.bfloat16
F32 = jnp.float32
I32 = jnp.int32
NT = (((1,), (1,)), ((), ()))
NN = (((1,), (0,)), ((), ()))
TN = (((0,), (0,)), ((), ()))

COLS = 64
NODES = 2048
DOM = 32
FEAT = 4
SLOTS = 256
TILE = 128
TILES = 96
LOCAL_TILES = 32
OWN_TILES = NODES // TILE
RECV_TILES = DOM * SLOTS // TILE
HALF = NODES // 2
HALF_TILES = OWN_TILES // 2
LOW = 256
HIGH = NODES // LOW
HUBS = 4096
HID = FEAT * COLS
EARLY = 2 * COLS + COLS // 2

SPARE_TILES = 576
SPARE_SUMS = 288
SPARE_ROWS = 2304
LIST = 1024
LISTS = 4608

SMEM = pl.BlockSpec(memory_space=pltpu.SMEM)
ANY = pl.BlockSpec(memory_space=pl.ANY)


def dot(a, b, dims):
    return lax.dot_general(a, b, dims, preferred_element_type=F32)


def shape(*dims, dtype=BF):
    return jax.ShapeDtypeStruct(dims, dtype)


VMEM = pl.BlockSpec(memory_space=pltpu.VMEM)


def local_call(kernel, outs, args, name, places=(), scratch=(), flops=10**9, size=2**21, mib=14):
    places = dict(places)
    return pl.pallas_call(
        kernel,
        out_shape=outs,
        in_specs=[places.get(i, VMEM) for i in range(len(args))],
        out_specs=[places.get(100 + i, SMEM if o.dtype == I32 else VMEM) for i, o in enumerate(outs)],
        scratch_shapes=list(scratch),
        compiler_params=pltpu.CompilerParams(vmem_limit_bytes=mib * 1024 * 1024),
        cost_estimate=pl.CostEstimate(flops=flops, bytes_accessed=size, transcendentals=0),
        name=name,
    )(*args)


def one_hot(low):
    rows = lax.broadcasted_iota(I32, (LOW, low.shape[1]), 0)
    return jnp.where(rows == low, 1.0, 0.0).astype(BF)


def pack_kernel(feat_ref, x_ref, up_ref, self_ref, neigh_ref, keep_ref, send_ref):
    for k, out in enumerate((keep_ref, send_ref)):
        lanes = pl.ds(pl.multiple_of((feat_ref[0] ^ k) * HALF, HALF), HALF)
        out[:COLS] = x_ref[:, lanes]
        out[COLS : 2 * COLS] = up_ref[:, lanes]
        for part in range(2):
            half = slice(part * COLS // 2, (part + 1) * COLS // 2)
            out[2 * COLS :, 2 * part * HID : (2 * part + 1) * HID] = self_ref[half]
            out[2 * COLS :, (2 * part + 1) * HID : (2 * part + 2) * HID] = neigh_ref[half]


def pack(feat, x, up, self_weight, neigh_weight):
    return local_call(
        pack_kernel,
        [shape(EARLY, HALF)] * 2,
        [feat, x, up, self_weight, neigh_weight],
        "pack",
        places={0: SMEM},
        flops=0,
        mib=60,
    )


def gather_kernel(x_ref, slot_ref, hub_ref, out_ref, stacked):
    for b in range(HIGH):
        stacked[b * COLS : (b + 1) * COLS, :] = x_ref[:, b * LOW : (b + 1) * LOW]

    @pl.loop(0, DOM, unroll=16)
    def _(r):
        index = slot_ref[pl.ds(r, 1), :]
        high = index >> 8
        found = dot(stacked[...], one_hot(index & (LOW - 1)), NN)
        out = jnp.zeros((COLS, SLOTS), F32)
        for b in range(HIGH):
            out = jnp.where(high == b, found[b * COLS : (b + 1) * COLS], out)
        out = out.astype(BF)
        out_ref[r, 0] = out[:, :TILE]
        out_ref[r, 1] = out[:, TILE:]
        out_ref[r, 2] = hub_ref[...]


def gather_rows(x, slots, hubs):
    return local_call(
        gather_kernel,
        [shape(DOM, 3, COLS, TILE)],
        [x, slots, hubs],
        "gather_rows",
        scratch=[pltpu.VMEM((HIGH * COLS, LOW), BF)],
        flops=4 * 10**9,
        mib=60,
    )[0]


def prepare_kernel(index_ref, x_ref, tile_hbm, list_hbm, sorted_hbm, total_hbm, list_ref, total_ref, tile_ref, sems):
    copy = pltpu.make_async_copy(tile_hbm, tile_ref, sems.at[0])
    copy.start()
    copy.wait()

    def sort(c, count):
        source = index_ref[1, c]
        own = source < OWN_TILES
        to = jnp.where(own, RECV_TILES + jnp.minimum(count, LOCAL_TILES - 1), source - OWN_TILES)
        list_ref[to] = index_ref[0, c]
        list_ref[TILES + to] = c
        pltpu.make_async_copy(tile_ref.at[c], sorted_hbm.at[to], sems.at[1]).start()
        return count + own.astype(I32)

    lax.fori_loop(0, TILES, sort, jnp.int32(0))
    total_ref[...] = jnp.zeros_like(total_ref)
    group = 8

    @pl.loop(0, LOCAL_TILES // group)
    def _(g):
        products = []
        for k in range(group):
            place = RECV_TILES + g * group + k
            c = list_ref[TILES + place]
            s = jnp.minimum(index_ref[1, c], OWN_TILES - 1)
            list_ref[TILES + place] = s
            lanes = pl.ds(pl.multiple_of(s * TILE, TILE), TILE)
            products.append(dot(tile_ref[c], x_ref[:, lanes], NT))
        for k in range(group):
            d = list_ref[RECV_TILES + g * group + k]
            total_ref[d] = total_ref[d] + products[k]

    outs = [
        pltpu.make_async_copy(total_ref, total_hbm.at[pl.ds(0, OWN_TILES)], sems.at[2]),
        pltpu.make_async_copy(list_ref, list_hbm.at[0], sems.at[3]),
    ]
    for copy in outs:
        copy.start()
    for copy in outs:
        copy.wait()
    pltpu.make_async_copy(tile_ref, sorted_hbm.at[pl.ds(0, TILES)], sems.at[1]).wait()


def prepare(index, x, tiles):
    return local_call(
        prepare_kernel,
        [
            shape(LISTS, LIST, dtype=I32),
            shape(SPARE_TILES, TILE, TILE),
            shape(SPARE_SUMS, TILE, COLS, dtype=F32),
        ],
        [index, x, tiles],
        "prepare",
        places={0: SMEM, 2: ANY, 100: ANY, 101: ANY, 102: ANY},
        scratch=[
            pltpu.SMEM((LIST,), I32),
            pltpu.VMEM((OWN_TILES, TILE, COLS), F32),
            pltpu.VMEM((TILES, TILE, TILE), BF),
            pltpu.SemaphoreType.DMA((4,)),
        ],
        mib=60,
    )


HUB_STEPS = 4
HALF_ROWS = HALF // HUB_STEPS


def hub_row_copies(half, hub_hbm, hub_ref, sems):
    copies = []
    for i in range(HUB_STEPS):
        rows = pl.ds(pl.multiple_of(half * HALF + i * HALF_ROWS, HALF_ROWS), HALF_ROWS)
        part = pl.ds(i * HALF_ROWS, HALF_ROWS)
        copies.append(pltpu.make_async_copy(hub_hbm.at[rows], hub_ref.at[part], sems.at[i]))
    return copies


def add_hub_rows(copies, hub_ref, hubs, total, first_tile):
    tiles = HALF_ROWS // TILE
    for step in range(HUB_STEPS):
        copies[step].wait()
        part = dot(hub_ref[step * HALF_ROWS : (step + 1) * HALF_ROWS], hubs[...], NT)
        for k in range(tiles):
            t = first_tile + step * tiles + k
            total[t] = total[t] + part[k * TILE : (k + 1) * TILE]


def forward_send_kernel(feat_ref, list_hbm, recv_ref, tile_hbm, local_hbm, hub_hbm, *rest):
    send_ref, keep_ref, hubs, target_ref, tile_ref, total, hub_ref, sems = rest
    away = 1 - feat_ref[0]
    tile_copy = pltpu.make_async_copy(tile_hbm.at[pl.ds(0, RECV_TILES)], tile_ref, sems.at[HUB_STEPS])
    local_copy = pltpu.make_async_copy(local_hbm.at[pl.ds(0, OWN_TILES)], total, sems.at[HUB_STEPS + 1])
    list_copy = pltpu.make_async_copy(list_hbm.at[0], target_ref, sems.at[HUB_STEPS + 2])
    copies = hub_row_copies(away, hub_hbm, hub_ref, sems)
    for copy in (list_copy, tile_copy, local_copy):
        copy.start()
    for q in range(DOM):
        hubs[:, q * TILE : (q + 1) * TILE] = recv_ref[q, 2]
    for copy in copies:
        copy.start()
    list_copy.wait()
    tile_copy.wait()
    local_copy.wait()
    group = 16

    @pl.loop(0, RECV_TILES // group)
    def _(step):
        first = step * group
        products = [dot(tile_ref[first + k], recv_ref[first // 2 + k // 2, k % 2], NT) for k in range(group)]
        for k, product in enumerate(products):
            d = target_ref[first + k]
            total[d] = total[d] + product

    add_hub_rows(copies, hub_ref, hubs, total, away * HALF_TILES)
    for j in range(HALF_TILES):
        send_ref[:, j * TILE : (j + 1) * TILE] = total[away * HALF_TILES + j].T.astype(BF)
        keep_ref[j] = total[feat_ref[0] * HALF_TILES + j]


def forward_send(feat, target, recv, tiles, local, hub_coef):
    return local_call(
        forward_send_kernel,
        [shape(COLS, HALF), shape(HALF_TILES, TILE, COLS, dtype=F32), shape(COLS, HUBS)],
        [feat, target, recv, tiles, local, hub_coef],
        "forward_send",
        places={0: SMEM, 1: ANY, 3: ANY, 4: ANY, 5: ANY},
        scratch=[
            pltpu.SMEM((LIST,), I32),
            pltpu.VMEM((RECV_TILES, TILE, TILE), BF),
            pltpu.VMEM((OWN_TILES, TILE, COLS), F32),
            pltpu.VMEM((HALF, HUBS), BF),
            pltpu.SemaphoreType.DMA((HUB_STEPS + 3,)),
        ],
        flops=2 * 10**9,
        size=2**23,
        mib=47,
    )


def forward_keep_kernel(feat_ref, sum_ref, hubs, hub_hbm, keep_ref, total, hub_ref, sems):
    copies = hub_row_copies(feat_ref[0], hub_hbm, hub_ref, sems)
    for copy in copies:
        copy.start()
    total[...] = sum_ref[...]
    add_hub_rows(copies, hub_ref, hubs, total, 0)
    for j in range(HALF_TILES):
        keep_ref[:, j * TILE : (j + 1) * TILE] = total[j].T.astype(BF)


def forward_keep(feat, sums, hubs, hub_coef):
    return local_call(
        forward_keep_kernel,
        [shape(COLS, HALF)],
        [feat, sums, hubs, hub_coef],
        "forward_keep",
        places={0: SMEM, 3: ANY},
        scratch=[
            pltpu.VMEM(sums.shape, F32),
            pltpu.VMEM((HALF, HUBS), BF),
            pltpu.SemaphoreType.DMA((HUB_STEPS,)),
        ],
        size=2**23,
        mib=47,
    )[0]


def rows_of(feat_ref, k):
    return pl.ds(pl.multiple_of((feat_ref[0] * 2 + feat_ref[1] ^ k) * COLS, COLS), COLS)


def dense_kernel(feat_ref, *rest):
    aggs, earlies, outs, scratch = rest[:4], rest[4:8], rest[8:14], rest[14:]
    keep_grad, send_grad, grad_ref, self_ref, keep_out, send_out = outs
    agg, x, up, neigh_ref, output = scratch
    for k in range(FEAT):
        rows = rows_of(feat_ref, k)
        agg[rows] = aggs[k][...]
        x[rows] = earlies[k][:COLS]
        up[rows] = earlies[k][COLS : 2 * COLS]
        for part in range(2):
            packed = earlies[k][2 * COLS :, part * 2 * HID : (part + 1) * 2 * HID]
            first = (feat_ref[0] * 2 + feat_ref[1] ^ k) * COLS + part * COLS // 2
            half = pl.ds(pl.multiple_of(first, COLS // 2), COLS // 2)
            self_ref[half] = packed[:, :HID]
            neigh_ref[half] = packed[:, HID:]
    pre_act = dot(self_ref[...], x[...], TN) + dot(neigh_ref[...], agg[...], TN)
    fall = jnp.exp(jnp.minimum(pre_act, 0.0))
    output[...] = jnp.where(pre_act > 0, pre_act, fall - 1.0).astype(BF)
    slope = jnp.where(pre_act > 0, 1.0, fall)
    grad_pre = (up[...].astype(F32) * slope).astype(BF)
    grad_ref[...] = grad_pre
    weight = jnp.concatenate([neigh_ref[rows_of(feat_ref, 0)], neigh_ref[rows_of(feat_ref, 2)]], 0)
    grad_agg = dot(weight, grad_pre, NN).astype(BF)
    keep_grad[...] = grad_agg[:COLS]
    send_grad[...] = grad_agg[COLS:]
    keep_out[...] = output[rows_of(feat_ref, 0)]
    send_out[...] = output[rows_of(feat_ref, 2)]


def dense(feat, aggs, earlies):
    block = pltpu.VMEM((HID, HALF), BF)
    return local_call(
        dense_kernel,
        [shape(COLS, HALF)] * 2 + [shape(HID, HALF), shape(HID, HID)] + [shape(COLS, HALF)] * 2,
        [feat, *aggs, *earlies],
        "dense",
        places={0: SMEM},
        scratch=[block] * 3 + [pltpu.VMEM((HID, HID), BF), block],
    )


HUB_LANES = HUBS // HUB_STEPS


def hub_lane_copies(half, hub_hbm, hub_ref, sems):
    rows = pl.ds(pl.multiple_of(half * HALF, HALF), HALF)
    copies = []
    for i in range(HUB_STEPS):
        lanes = pl.ds(i * HUB_LANES, HUB_LANES)
        copies.append(pltpu.make_async_copy(hub_hbm.at[rows, lanes], hub_ref.at[:, lanes], sems.at[i]))
    return copies


def hub_backward_kernel(feat_ref, grad_ref, self_ref, pre_ref, hub_hbm, *rest):
    out_ref, keep_back, send_back, hub_ref, sems = rest
    copies = hub_lane_copies(feat_ref[0], hub_hbm, hub_ref, sems)
    for copy in copies:
        copy.start()
    weight = jnp.concatenate([self_ref[rows_of(feat_ref, 0)], self_ref[rows_of(feat_ref, 2)]], 0)
    back = dot(weight, pre_ref[...], NN).astype(BF)
    keep_back[...] = back[:COLS]
    send_back[...] = back[COLS:]
    for i, copy in enumerate(copies):
        copy.wait()
        lanes = slice(i * HUB_LANES, (i + 1) * HUB_LANES)
        out_ref[:, lanes] = dot(grad_ref[...], hub_ref[:, lanes], NN)


def hub_backward(feat, grad, self_weight, grad_pre, hub_coef):
    return local_call(
        hub_backward_kernel,
        [shape(COLS, HUBS, dtype=F32), shape(COLS, HALF), shape(COLS, HALF)],
        [feat, grad, self_weight, grad_pre, hub_coef],
        "hub_backward",
        places={0: SMEM, 4: ANY},
        scratch=[pltpu.VMEM((HALF, HUBS), BF), pltpu.SemaphoreType.DMA((HUB_STEPS,))],
        size=2**23,
        mib=47,
    )


def split_tiles(feat_ref, keep_ref, come_ref, grads):
    for k, part in enumerate((keep_ref, come_ref)):
        first = (feat_ref[0] ^ k) * HALF_TILES
        for j in range(HALF_TILES):
            grads[first + j] = part[:, j * TILE : (j + 1) * TILE]


def backward_kernel(feat_ref, list_hbm, keep_ref, come_ref, terms_hbm, tile_hbm, hub_hbm, *rest):
    out_ref, target_ref, grads, terms_ref, tile_ref, hub_ref, sems = rest
    group = RECV_TILES // HUB_STEPS
    doms = DOM // HUB_STEPS
    hub_parts = hub_lane_copies(1 - feat_ref[0], hub_hbm, hub_ref, sems)
    tile_parts, term_parts = [], []
    for i in range(HUB_STEPS):
        part = pl.ds(i * group, group)
        tile_parts.append(pltpu.make_async_copy(tile_hbm.at[part], tile_ref.at[part], sems.at[HUB_STEPS + i]))
        lanes = pl.ds(i * HUB_LANES, HUB_LANES)
        term_parts.append(
            pltpu.make_async_copy(terms_hbm.at[:, lanes], terms_ref.at[:, lanes], sems.at[2 * HUB_STEPS + i])
        )
    list_copy = pltpu.make_async_copy(list_hbm.at[0], target_ref, sems.at[3 * HUB_STEPS])
    list_copy.start()
    for copies in zip(tile_parts, hub_parts, term_parts):
        for copy in copies:
            copy.start()
    split_tiles(feat_ref, keep_ref, come_ref, grads)
    list_copy.wait()
    for step in range(HUB_STEPS):
        tile_parts[step].wait()
        for s in range(step * group, (step + 1) * group):
            out_ref[s // 2, s % 2] = dot(grads[target_ref[s]], tile_ref[s], NN).astype(BF)
        hub_parts[step].wait()
        term_parts[step].wait()
        lanes = slice(step * HUB_LANES, (step + 1) * HUB_LANES)
        terms = (terms_ref[:, lanes] + dot(come_ref[...], hub_ref[:, lanes], NN)).astype(BF)
        for k in range(doms):
            out_ref[step * doms + k, 2] = terms[:, k * TILE : (k + 1) * TILE]


def backward(feat, target, keep, come, terms, tiles, hub_coef):
    return local_call(
        backward_kernel,
        [shape(DOM, 3, COLS, TILE)],
        [feat, target, keep, come, terms, tiles, hub_coef],
        "backward",
        places={0: SMEM, 1: ANY, 4: ANY, 5: ANY, 6: ANY},
        scratch=[
            pltpu.SMEM((LIST,), I32),
            pltpu.VMEM((OWN_TILES, COLS, TILE), BF),
            pltpu.VMEM((COLS, HUBS), F32),
            pltpu.VMEM((RECV_TILES, TILE, TILE), BF),
            pltpu.VMEM((HALF, HUBS), BF),
            pltpu.SemaphoreType.DMA((3 * HUB_STEPS + 1,)),
        ],
        flops=2 * 10**9,
        size=2**23,
        mib=47,
    )[0]


def own_backward_kernel(feat_ref, list_hbm, keep_ref, come_ref, tile_hbm, own_hbm, *rest):
    list_ref, own_ref, grads, total, tile_ref, sems = rest
    copies = [
        pltpu.make_async_copy(list_hbm.at[0], list_ref, sems.at[0]),
        pltpu.make_async_copy(tile_hbm.at[pl.ds(RECV_TILES, LOCAL_TILES)], tile_ref, sems.at[1]),
    ]
    for copy in copies:
        copy.start()
    split_tiles(feat_ref, keep_ref, come_ref, grads)
    total[...] = jnp.zeros_like(total)
    for copy in copies:
        copy.wait()
    group = 8

    @pl.loop(0, LOCAL_TILES // group)
    def _(g):
        places = [RECV_TILES + g * group + k for k in range(group)]
        products = [dot(grads[list_ref[c]], tile_ref[c - RECV_TILES], NN) for c in places]
        for c, product in zip(places, products):
            s = list_ref[TILES + c]
            total[s] = total[s] + product

    for t in range(OWN_TILES):
        own_ref[:, t * TILE : (t + 1) * TILE] = total[t]
    out_copy = pltpu.make_async_copy(own_ref, own_hbm.at[pl.ds(0, COLS)], sems.at[2])
    out_copy.start()
    out_copy.wait()


def own_backward(feat, lists, keep, come, tiles):
    return local_call(
        own_backward_kernel,
        [shape(SPARE_ROWS, NODES, dtype=F32)],
        [feat, lists, keep, come, tiles],
        "own_backward",
        places={0: SMEM, 1: ANY, 4: ANY, 100: ANY},
        scratch=[
            pltpu.SMEM((LIST,), I32),
            pltpu.VMEM((COLS, NODES), F32),
            pltpu.VMEM((OWN_TILES, COLS, TILE), BF),
            pltpu.VMEM((OWN_TILES, COLS, TILE), F32),
            pltpu.VMEM((LOCAL_TILES, TILE, TILE), BF),
            pltpu.SemaphoreType.DMA((3,)),
        ],
        mib=60,
    )[0]


def scatter_kernel(feat_ref, slot_ref, recv_ref, own_hbm, keep_ref, come_ref, out_keep, out_come, *rest):
    grad_ref, hub_ref, output_ref, total, own_ref, sems = rest
    own_copy = pltpu.make_async_copy(own_hbm.at[pl.ds(0, COLS)], own_ref, sems.at[0])
    own_copy.start()
    total[...] = jnp.zeros_like(total)
    group = 16

    @pl.loop(0, DOM // group)
    def _(g):
        spread, hots = [], []
        for k in range(group):
            r = g * group + k
            index = slot_ref[pl.ds(r, 1), :]
            high = index >> 8
            rows = jnp.concatenate([recv_ref[r, 0], recv_ref[r, 1]], 1)
            spread.append(
                jnp.concatenate([jnp.where(high == b, rows, jnp.zeros_like(rows)) for b in range(HIGH)], 0)
            )
            hots.append(one_hot(index & (LOW - 1)))
        total[...] += dot(jnp.concatenate(spread, 1), jnp.concatenate(hots, 1), NT)

    hub = jnp.zeros((COLS, TILE), F32)
    for r in range(DOM):
        hub = hub + recv_ref[r, 2].astype(F32)
    hub_ref[...] = hub
    own_copy.wait()
    for b in range(HIGH):
        lanes = slice(b * LOW, (b + 1) * LOW)
        grad_ref[:, lanes] = total[b * COLS : (b + 1) * COLS] + own_ref[:, lanes]
    keep = pl.ds(pl.multiple_of(feat_ref[0] * HALF, HALF), HALF)
    come = pl.ds(pl.multiple_of((1 - feat_ref[0]) * HALF, HALF), HALF)
    grad_ref[:, keep] = grad_ref[:, keep] + keep_ref[...].astype(F32)
    grad_ref[:, come] = grad_ref[:, come] + come_ref[...].astype(F32)
    output_ref[:, keep] = out_keep[...]
    output_ref[:, come] = out_come[...]


def scatter_rows(feat, slots, recv, own, keep, come, out_keep, out_come):
    return local_call(
        scatter_kernel,
        [shape(COLS, NODES, dtype=F32), shape(COLS, TILE, dtype=F32), shape(COLS, NODES)],
        [feat, slots, recv, own, keep, come, out_keep, out_come],
        "scatter_rows",
        places={0: SMEM, 3: ANY},
        scratch=[
            pltpu.VMEM((HIGH * COLS, LOW), F32),
            pltpu.VMEM((COLS, NODES), F32),
            pltpu.SemaphoreType.DMA((1,)),
        ],
        mib=47,
    )


def to_dom(x):
    return lax.all_to_all(x, "dom", split_axis=0, concat_axis=0, tiled=True)


def swap(x, k):
    return lax.ppermute(x, "feat", [(f, f ^ k) for f in range(FEAT)])


def after(x, *others):
    return lax.optimization_barrier((x, *others))[0]


def body(
    features,
    hub_feats,
    hub_coef,
    tile_coef,
    tile_index,
    boundary_rows,
    self_weight,
    neigh_weight,
    out_grad,
):
    x = features.T
    up = out_grad.T
    slots = boundary_rows[0]
    index = tile_index.T
    place = lax.axis_index("feat")
    high = place // 2
    feat = jnp.stack([high, place % 2])

    outgoing = gather_rows(x, slots, hub_feats.T)
    incoming = to_dom(outgoing)
    x_in, up_in = lax.optimization_barrier((x, up, outgoing))[:2]
    early, early_send = pack(feat, x_in, up_in, self_weight, neigh_weight)
    early_2 = swap(early_send, 2)
    early_1 = swap(early, 1)
    lists, tiles, local_sum = prepare(index, x_in, tile_coef)
    agg_send, sums, hubs = forward_send(feat, lists, incoming, tiles, local_sum, hub_coef)
    agg_2 = swap(agg_send, 2)
    early_2 = after(early_2, agg_send)
    early = [early, early_1, early_2, swap(early_2, 1)]
    agg = forward_keep(feat, sums, hubs, hub_coef)
    grad, grad_send, grad_pre, self_weight, out_keep, out_send = dense(
        feat, [agg, swap(agg, 1), agg_2, swap(agg_2, 1)], early
    )
    grad_2 = swap(grad_send, 2)
    terms, back, back_send = hub_backward(feat, grad, self_weight, grad_pre, hub_coef)
    grad_2, back_send, out_send = lax.optimization_barrier((grad_2, back_send, out_send))
    back_2 = swap(back_send, 2)
    sums = backward(feat, lists, grad, grad_2, terms, tiles, hub_coef)
    sums, back_2, out_send = lax.optimization_barrier((sums, back_2, out_send))
    returned = to_dom(sums)
    out_2 = swap(out_send, 2)
    own_grad = own_backward(feat, lists, after(grad, sums), grad_2, tiles)
    grad_feats, grad_hubs, output_rows = scatter_rows(
        feat, slots, returned, own_grad, back, back_2, out_keep, out_2
    )
    return (output_rows.T, grad_feats.T, grad_hubs.T)


def solution(mesh):
    return jax.shard_map(
        body,
        mesh=mesh,
        in_specs=(
            P("dom", "feat"),
            P("dom", "feat"),
            P("dom", None),
            P("dom", None, None),
            P("dom", None),
            P("dom", None, None),
            P("feat", None),
            P("feat", None),
            P("dom", "feat"),
        ),
        out_specs=(P("dom", "feat"), P("dom", "feat"), P("dom", "feat")),
        check_vma=False,
    )
```

```python
import jax
import jax.numpy as jnp
from jax import lax
from jax.experimental import pallas as pl
from jax.experimental.pallas import tpu as pltpu
from jax.sharding import PartitionSpec as P

BF = jnp.bfloat16
F32 = jnp.float32
I32 = jnp.int32
NT = (((1,), (1,)), ((), ()))
NN = (((1,), (0,)), ((), ()))
TN = (((0,), (0,)), ((), ()))

COLS = 64
NODES = 2048
DOM = 32
FEAT = 4
SLOTS = 256
TILE = 128
TILES = 96
LOCAL_TILES = 32
OWN_TILES = NODES // TILE
RECV_TILES = DOM * SLOTS // TILE
HALF = NODES // 2
HALF_TILES = OWN_TILES // 2
LOW = 256
HIGH = NODES // LOW
HUBS = 4096
HID = FEAT * COLS
EARLY = 2 * COLS + COLS // 2

SPARE_TILES = 576
SPARE_SUMS = 288
SPARE_ROWS = 2304
LIST = 1024
LISTS = 4608

SMEM = pl.BlockSpec(memory_space=pltpu.SMEM)
ANY = pl.BlockSpec(memory_space=pl.ANY)


def dot(a, b, dims):
    return lax.dot_general(a, b, dims, preferred_element_type=F32)


def shape(*dims, dtype=BF):
    return jax.ShapeDtypeStruct(dims, dtype)


VMEM = pl.BlockSpec(memory_space=pltpu.VMEM)


def local_call(kernel, outs, args, name, places=(), scratch=(), flops=10**9, size=2**21, mib=14):
    places = dict(places)
    return pl.pallas_call(
        kernel,
        out_shape=outs,
        in_specs=[places.get(i, VMEM) for i in range(len(args))],
        out_specs=[places.get(100 + i, SMEM if o.dtype == I32 else VMEM) for i, o in enumerate(outs)],
        scratch_shapes=list(scratch),
        compiler_params=pltpu.CompilerParams(vmem_limit_bytes=mib * 1024 * 1024),
        cost_estimate=pl.CostEstimate(flops=flops, bytes_accessed=size, transcendentals=0),
        name=name,
    )(*args)


def one_hot(low):
    rows = lax.broadcasted_iota(I32, (LOW, low.shape[1]), 0)
    return jnp.where(rows == low, 1.0, 0.0).astype(BF)


def pack_kernel(x_ref, up_ref, self_ref, neigh_ref, keep_ref, send_ref):
    for k, out in enumerate((keep_ref, send_ref)):
        lanes = pl.ds(pl.multiple_of((chip() ^ k) * HALF, HALF), HALF)
        out[:COLS] = x_ref[:, lanes]
        out[COLS : 2 * COLS] = up_ref[:, lanes]
        for part in range(2):
            half = slice(part * COLS // 2, (part + 1) * COLS // 2)
            out[2 * COLS :, 2 * part * HID : (2 * part + 1) * HID] = self_ref[half]
            out[2 * COLS :, (2 * part + 1) * HID : (2 * part + 2) * HID] = neigh_ref[half]


def pack(x, up, self_weight, neigh_weight):
    return local_call(
        pack_kernel,
        [shape(EARLY, HALF)] * 2,
        [x, up, self_weight, neigh_weight],
        "pack",
        places={},
        flops=0,
        mib=60,
    )


def gather_kernel(x_ref, slot_ref, hub_ref, out_ref, stacked):
    for b in range(HIGH):
        stacked[b * COLS : (b + 1) * COLS, :] = x_ref[:, b * LOW : (b + 1) * LOW]

    @pl.loop(0, DOM, unroll=16)
    def _(r):
        index = slot_ref[pl.ds(r, 1), :]
        high = index >> 8
        found = dot(stacked[...], one_hot(index & (LOW - 1)), NN)
        out = jnp.zeros((COLS, SLOTS), F32)
        for b in range(HIGH):
            out = jnp.where(high == b, found[b * COLS : (b + 1) * COLS], out)
        out = out.astype(BF)
        out_ref[r, 0] = out[:, :TILE]
        out_ref[r, 1] = out[:, TILE:]
        out_ref[r, 2] = hub_ref[...]


def gather_rows(x, slots, hubs):
    return local_call(
        gather_kernel,
        [shape(DOM, 3, COLS, TILE)],
        [x, slots, hubs],
        "gather_rows",
        scratch=[pltpu.VMEM((HIGH * COLS, LOW), BF)],
        flops=4 * 10**9,
        mib=60,
    )[0]


def prepare_kernel(index_ref, x_ref, tile_hbm, list_hbm, sorted_hbm, total_hbm, list_ref, total_ref, tile_ref, sems):
    copy = pltpu.make_async_copy(tile_hbm, tile_ref, sems.at[0])
    copy.start()
    copy.wait()

    def sort(c, count):
        source = index_ref[1, c]
        own = source < OWN_TILES
        to = jnp.where(own, RECV_TILES + jnp.minimum(count, LOCAL_TILES - 1), source - OWN_TILES)
        list_ref[to] = index_ref[0, c]
        list_ref[TILES + to] = c
        pltpu.make_async_copy(tile_ref.at[c], sorted_hbm.at[to], sems.at[1]).start()
        return count + own.astype(I32)

    lax.fori_loop(0, TILES, sort, jnp.int32(0))
    total_ref[...] = jnp.zeros_like(total_ref)
    group = 8

    @pl.loop(0, LOCAL_TILES // group)
    def _(g):
        products = []
        for k in range(group):
            place = RECV_TILES + g * group + k
            c = list_ref[TILES + place]
            s = jnp.minimum(index_ref[1, c], OWN_TILES - 1)
            list_ref[TILES + place] = s
            lanes = pl.ds(pl.multiple_of(s * TILE, TILE), TILE)
            products.append(dot(tile_ref[c], x_ref[:, lanes], NT))
        for k in range(group):
            d = list_ref[RECV_TILES + g * group + k]
            total_ref[d] = total_ref[d] + products[k]

    outs = [
        pltpu.make_async_copy(total_ref, total_hbm.at[pl.ds(0, OWN_TILES)], sems.at[2]),
        pltpu.make_async_copy(list_ref, list_hbm.at[0], sems.at[3]),
    ]
    for copy in outs:
        copy.start()
    for copy in outs:
        copy.wait()
    pltpu.make_async_copy(tile_ref, sorted_hbm.at[pl.ds(0, TILES)], sems.at[1]).wait()


def prepare(index, x, tiles):
    return local_call(
        prepare_kernel,
        [
            shape(LISTS, LIST, dtype=I32),
            shape(SPARE_TILES, TILE, TILE),
            shape(SPARE_SUMS, TILE, COLS, dtype=F32),
        ],
        [index, x, tiles],
        "prepare",
        places={0: SMEM, 2: ANY, 100: ANY, 101: ANY, 102: ANY},
        scratch=[
            pltpu.SMEM((LIST,), I32),
            pltpu.VMEM((OWN_TILES, TILE, COLS), F32),
            pltpu.VMEM((TILES, TILE, TILE), BF),
            pltpu.SemaphoreType.DMA((4,)),
        ],
        mib=60,
    )


HUB_STEPS = 4
HALF_ROWS = HALF // HUB_STEPS


def half_rows(half, step):
    return pl.ds(pl.multiple_of(half * HALF + step * HALF_ROWS, HALF_ROWS), HALF_ROWS)


def add_hub_rows(hub_ref, half, step, hubs, total, first_tile):
    tiles = HALF_ROWS // TILE
    part = dot(hub_ref[half_rows(half, step)], hubs[...], NT)
    for k in range(tiles):
        t = first_tile + step * tiles + k
        total[t] = total[t] + part[k * TILE : (k + 1) * TILE]


def forward_send_kernel(list_hbm, recv_ref, tile_hbm, local_hbm, hub_hbm, *rest):
    send_ref, keep_ref, hubs, hub_ref, target_ref, tile_ref, total, sems = rest
    away = 1 - chip()
    firsts = [
        pltpu.make_async_copy(src, dst, sems.at[2 * HUB_STEPS + i])
        for i, (src, dst) in enumerate(
            (
                (list_hbm.at[0], target_ref),
                (tile_hbm.at[pl.ds(0, RECV_TILES)], tile_ref),
                (local_hbm.at[pl.ds(0, OWN_TILES)], total),
            )
        )
    ]
    copies = []
    for h, half in enumerate((away, chip())):
        for i in range(HUB_STEPS):
            rows = half_rows(half, i)
            copies.append(pltpu.make_async_copy(hub_hbm.at[rows], hub_ref.at[rows], sems.at[h * HUB_STEPS + i]))
    for copy in firsts + copies:
        copy.start()
    for q in range(DOM):
        hubs[:, q * TILE : (q + 1) * TILE] = recv_ref[q, 2]
    for copy in firsts:
        copy.wait()
    group = 16

    @pl.loop(0, RECV_TILES // group)
    def _(step):
        first = step * group
        products = [dot(tile_ref[first + k], recv_ref[first // 2 + k // 2, k % 2], NT) for k in range(group)]
        for k, product in enumerate(products):
            d = target_ref[first + k]
            total[d] = total[d] + product

    for step in range(HUB_STEPS):
        copies[step].wait()
        add_hub_rows(hub_ref, away, step, hubs, total, away * HALF_TILES)
    for j in range(HALF_TILES):
        send_ref[:, j * TILE : (j + 1) * TILE] = total[away * HALF_TILES + j].T.astype(BF)
        keep_ref[j] = total[chip() * HALF_TILES + j]
    for copy in copies[HUB_STEPS:]:
        copy.wait()


def forward_send(lists, recv, tiles, local, hub_coef):
    return local_call(
        forward_send_kernel,
        [
            shape(COLS, HALF),
            shape(HALF_TILES, TILE, COLS, dtype=F32),
            shape(COLS, HUBS),
            shape(NODES, HUBS),
        ],
        [lists, recv, tiles, local, hub_coef],
        "forward_send",
        places={0: ANY, 2: ANY, 3: ANY, 4: ANY},
        scratch=[
            pltpu.SMEM((LIST,), I32),
            pltpu.VMEM((RECV_TILES, TILE, TILE), BF),
            pltpu.VMEM((OWN_TILES, TILE, COLS), F32),
            pltpu.SemaphoreType.DMA((2 * HUB_STEPS + 3,)),
        ],
        flops=2 * 10**9,
        size=2**24,
        mib=34,
    )


def forward_keep_kernel(sum_ref, hubs, hub_ref, keep_ref, total):
    total[...] = sum_ref[...]
    for step in range(HUB_STEPS):
        add_hub_rows(hub_ref, chip(), step, hubs, total, 0)
    for j in range(HALF_TILES):
        keep_ref[:, j * TILE : (j + 1) * TILE] = total[j].T.astype(BF)


def forward_keep(sums, hubs, hub):
    return local_call(
        forward_keep_kernel,
        [shape(COLS, HALF)],
        [sums, hubs, hub],
        "forward_keep",
        places={},
        scratch=[pltpu.VMEM(sums.shape, F32)],
        size=2**23,
        mib=20,
    )[0]


def chip():
    return lax.axis_index("feat") // 2


def rows_of(k):
    return pl.ds(pl.multiple_of((lax.axis_index("feat") ^ k) * COLS, COLS), COLS)


def dense_kernel(*rest):
    aggs, earlies, outs, scratch = rest[:4], rest[4:8], rest[8:14], rest[14:]
    keep_grad, send_grad, grad_ref, self_ref, keep_out, send_out = outs
    agg, x, up, neigh_ref, output = scratch
    for k in range(FEAT):
        rows = rows_of(k)
        agg[rows] = aggs[k][...]
        x[rows] = earlies[k][:COLS]
        up[rows] = earlies[k][COLS : 2 * COLS]
        for part in range(2):
            packed = earlies[k][2 * COLS :, part * 2 * HID : (part + 1) * 2 * HID]
            first = (lax.axis_index("feat") ^ k) * COLS + part * COLS // 2
            half = pl.ds(pl.multiple_of(first, COLS // 2), COLS // 2)
            self_ref[half] = packed[:, :HID]
            neigh_ref[half] = packed[:, HID:]
    pre_act = dot(self_ref[...], x[...], TN) + dot(neigh_ref[...], agg[...], TN)
    fall = jnp.exp(jnp.minimum(pre_act, 0.0))
    output[...] = jnp.where(pre_act > 0, pre_act, fall - 1.0).astype(BF)
    slope = jnp.where(pre_act > 0, 1.0, fall)
    grad_pre = (up[...].astype(F32) * slope).astype(BF)
    grad_ref[...] = grad_pre
    weight = jnp.concatenate([neigh_ref[rows_of(0)], neigh_ref[rows_of(2)]], 0)
    grad_agg = dot(weight, grad_pre, NN).astype(BF)
    keep_grad[...] = grad_agg[:COLS]
    send_grad[...] = grad_agg[COLS:]
    keep_out[...] = output[rows_of(0)]
    send_out[...] = output[rows_of(2)]


def dense(aggs, earlies):
    block = pltpu.VMEM((HID, HALF), BF)
    return local_call(
        dense_kernel,
        [shape(COLS, HALF)] * 2 + [shape(HID, HALF), shape(HID, HID)] + [shape(COLS, HALF)] * 2,
        [*aggs, *earlies],
        "dense",
        places={},
        scratch=[block] * 3 + [pltpu.VMEM((HID, HID), BF), block],
    )


HUB_LANES = HUBS // HUB_STEPS


def hub_part(half, step):
    return pl.ds(pl.multiple_of(half * HALF, HALF), HALF), slice(step * HUB_LANES, (step + 1) * HUB_LANES)


def hub_backward_kernel(grad_ref, self_ref, pre_ref, hub_ref, out_ref, keep_back, send_back):
    weight = jnp.concatenate([self_ref[rows_of(0)], self_ref[rows_of(2)]], 0)
    back = dot(weight, pre_ref[...], NN).astype(BF)
    keep_back[...] = back[:COLS]
    send_back[...] = back[COLS:]
    for step in range(HUB_STEPS):
        rows, lanes = hub_part(chip(), step)
        out_ref[:, lanes] = dot(grad_ref[...], hub_ref[rows, lanes], NN)


def hub_backward(grad, self_weight, grad_pre, hub):
    return local_call(
        hub_backward_kernel,
        [shape(COLS, HUBS, dtype=F32), shape(COLS, HALF), shape(COLS, HALF)],
        [grad, self_weight, grad_pre, hub],
        "hub_backward",
        places={},
        size=2**23,
        mib=20,
    )


def split_tiles(keep_ref, come_ref, grads):
    for k, part in enumerate((keep_ref, come_ref)):
        first = (chip() ^ k) * HALF_TILES
        for j in range(HALF_TILES):
            grads[first + j] = part[:, j * TILE : (j + 1) * TILE]


def backward_kernel(list_hbm, keep_ref, come_ref, terms_ref, tile_hbm, hub_ref, *rest):
    out_ref, target_ref, grads, tile_ref, sems = rest
    group = RECV_TILES // HUB_STEPS
    doms = DOM // HUB_STEPS
    list_copy = pltpu.make_async_copy(list_hbm.at[0], target_ref, sems.at[HUB_STEPS])
    list_copy.start()
    copies = []
    for i in range(HUB_STEPS):
        part = pl.ds(i * group, group)
        copies.append(pltpu.make_async_copy(tile_hbm.at[part], tile_ref.at[part], sems.at[i]))
        copies[i].start()
    split_tiles(keep_ref, come_ref, grads)
    list_copy.wait()
    for step in range(HUB_STEPS):
        rows, lanes = hub_part(1 - chip(), step)
        terms = (terms_ref[:, lanes] + dot(come_ref[...], hub_ref[rows, lanes], NN)).astype(BF)
        for k in range(doms):
            out_ref[step * doms + k, 2] = terms[:, k * TILE : (k + 1) * TILE]
        copies[step].wait()
        for s in range(step * group, (step + 1) * group):
            out_ref[s // 2, s % 2] = dot(grads[target_ref[s]], tile_ref[s], NN).astype(BF)


def backward(lists, keep, come, terms, tiles, hub):
    return local_call(
        backward_kernel,
        [shape(DOM, 3, COLS, TILE)],
        [lists, keep, come, terms, tiles, hub],
        "backward",
        places={0: ANY, 4: ANY},
        scratch=[
            pltpu.SMEM((LIST,), I32),
            pltpu.VMEM((OWN_TILES, COLS, TILE), BF),
            pltpu.VMEM((RECV_TILES, TILE, TILE), BF),
            pltpu.SemaphoreType.DMA((HUB_STEPS + 1,)),
        ],
        flops=2 * 10**9,
        size=2**23,
        mib=20,
    )[0]


def own_backward_kernel(list_hbm, keep_ref, come_ref, tile_hbm, own_hbm, *rest):
    list_ref, own_ref, grads, total, tile_ref, sems = rest
    copies = [
        pltpu.make_async_copy(list_hbm.at[0], list_ref, sems.at[0]),
        pltpu.make_async_copy(tile_hbm.at[pl.ds(RECV_TILES, LOCAL_TILES)], tile_ref, sems.at[1]),
    ]
    for copy in copies:
        copy.start()
    split_tiles(keep_ref, come_ref, grads)
    total[...] = jnp.zeros_like(total)
    for copy in copies:
        copy.wait()
    group = 8

    @pl.loop(0, LOCAL_TILES // group)
    def _(g):
        places = [RECV_TILES + g * group + k for k in range(group)]
        products = [dot(grads[list_ref[c]], tile_ref[c - RECV_TILES], NN) for c in places]
        for c, product in zip(places, products):
            s = list_ref[TILES + c]
            total[s] = total[s] + product

    for t in range(OWN_TILES):
        own_ref[:, t * TILE : (t + 1) * TILE] = total[t]
    out_copy = pltpu.make_async_copy(own_ref, own_hbm.at[pl.ds(0, COLS)], sems.at[2])
    out_copy.start()
    out_copy.wait()


def own_backward(lists, keep, come, tiles):
    return local_call(
        own_backward_kernel,
        [shape(SPARE_ROWS, NODES, dtype=F32)],
        [lists, keep, come, tiles],
        "own_backward",
        places={0: ANY, 3: ANY, 100: ANY},
        scratch=[
            pltpu.SMEM((LIST,), I32),
            pltpu.VMEM((COLS, NODES), F32),
            pltpu.VMEM((OWN_TILES, COLS, TILE), BF),
            pltpu.VMEM((OWN_TILES, COLS, TILE), F32),
            pltpu.VMEM((LOCAL_TILES, TILE, TILE), BF),
            pltpu.SemaphoreType.DMA((3,)),
        ],
        mib=60,
    )[0]


def scatter_kernel(slot_ref, recv_ref, own_hbm, keep_ref, come_ref, out_keep, out_come, *rest):
    grad_ref, hub_ref, output_ref, total, own_ref, sems = rest
    own_copy = pltpu.make_async_copy(own_hbm.at[pl.ds(0, COLS)], own_ref, sems.at[0])
    own_copy.start()
    total[...] = jnp.zeros_like(total)
    group = 16

    @pl.loop(0, DOM // group)
    def _(g):
        spread, hots = [], []
        for k in range(group):
            r = g * group + k
            index = slot_ref[pl.ds(r, 1), :]
            high = index >> 8
            rows = jnp.concatenate([recv_ref[r, 0], recv_ref[r, 1]], 1)
            spread.append(
                jnp.concatenate([jnp.where(high == b, rows, jnp.zeros_like(rows)) for b in range(HIGH)], 0)
            )
            hots.append(one_hot(index & (LOW - 1)))
        total[...] += dot(jnp.concatenate(spread, 1), jnp.concatenate(hots, 1), NT)

    hub = jnp.zeros((COLS, TILE), F32)
    for r in range(DOM):
        hub = hub + recv_ref[r, 2].astype(F32)
    hub_ref[...] = hub
    own_copy.wait()
    for b in range(HIGH):
        lanes = slice(b * LOW, (b + 1) * LOW)
        grad_ref[:, lanes] = total[b * COLS : (b + 1) * COLS] + own_ref[:, lanes]
    keep = pl.ds(pl.multiple_of(chip() * HALF, HALF), HALF)
    come = pl.ds(pl.multiple_of((1 - chip()) * HALF, HALF), HALF)
    grad_ref[:, keep] = grad_ref[:, keep] + keep_ref[...].astype(F32)
    grad_ref[:, come] = grad_ref[:, come] + come_ref[...].astype(F32)
    output_ref[:, keep] = out_keep[...]
    output_ref[:, come] = out_come[...]


def scatter_rows(slots, recv, own, keep, come, out_keep, out_come):
    return local_call(
        scatter_kernel,
        [shape(COLS, NODES, dtype=F32), shape(COLS, TILE, dtype=F32), shape(COLS, NODES)],
        [slots, recv, own, keep, come, out_keep, out_come],
        "scatter_rows",
        places={2: ANY},
        scratch=[
            pltpu.VMEM((HIGH * COLS, LOW), F32),
            pltpu.VMEM((COLS, NODES), F32),
            pltpu.SemaphoreType.DMA((1,)),
        ],
        mib=47,
    )


def to_dom(x):
    return lax.all_to_all(x, "dom", split_axis=0, concat_axis=0, tiled=True)


def swap(x, k):
    return lax.ppermute(x, "feat", [(f, f ^ k) for f in range(FEAT)])


def after(x, *others):
    return lax.optimization_barrier((x, *others))[0]


def body(
    features,
    hub_feats,
    hub_coef,
    tile_coef,
    tile_index,
    boundary_rows,
    self_weight,
    neigh_weight,
    out_grad,
):
    x = features.T
    up = out_grad.T
    slots = boundary_rows[0]
    index = tile_index.T

    outgoing = gather_rows(x, slots, hub_feats.T)
    incoming = to_dom(outgoing)
    x_in, up_in = lax.optimization_barrier((x, up, outgoing))[:2]
    early, early_send = pack(x_in, up_in, self_weight, neigh_weight)
    early_2 = swap(early_send, 2)
    early_1 = swap(early, 1)
    lists, tiles, local_sum = prepare(index, x_in, tile_coef)
    agg_send, sums, hubs, hub = forward_send(lists, incoming, tiles, local_sum, hub_coef)
    agg_2 = swap(agg_send, 2)
    early_2 = after(early_2, agg_send)
    early = [early, early_1, early_2, swap(early_2, 1)]
    agg = forward_keep(sums, hubs, hub)
    grad, grad_send, grad_pre, self_weight, out_keep, out_send = dense(
        [agg, swap(agg, 1), agg_2, swap(agg_2, 1)], early
    )
    grad_2 = swap(grad_send, 2)
    terms, back, back_send = hub_backward(grad, self_weight, grad_pre, hub)
    back_2 = swap(back_send, 2)
    sums = backward(lists, grad, grad_2, terms, tiles, hub)
    sums, back_2, out_send = lax.optimization_barrier((sums, back_2, out_send))
    returned = to_dom(sums)
    out_2 = swap(out_send, 2)
    own_grad = own_backward(lists, after(grad, sums), grad_2, tiles)
    grad_feats, grad_hubs, output_rows = scatter_rows(
        slots, returned, own_grad, back, back_2, out_keep, out_2
    )
    return (output_rows.T, grad_feats.T, grad_hubs.T)


def solution(mesh):
    return jax.shard_map(
        body,
        mesh=mesh,
        in_specs=(
            P("dom", "feat"),
            P("dom", "feat"),
            P("dom", None),
            P("dom", None, None),
            P("dom", None),
            P("dom", None, None),
            P("feat", None),
            P("feat", None),
            P("dom", "feat"),
        ),
        out_specs=(P("dom", "feat"), P("dom", "feat"), P("dom", "feat")),
        check_vma=False,
    )
```

```python
import jax
import jax.numpy as jnp
from jax import lax
from jax.experimental import pallas as pl
from jax.experimental.pallas import tpu as pltpu
from jax.sharding import PartitionSpec as P

BF = jnp.bfloat16
F32 = jnp.float32
I32 = jnp.int32
NT = (((1,), (1,)), ((), ()))
NN = (((1,), (0,)), ((), ()))
TN = (((0,), (0,)), ((), ()))

COLS = 64
NODES = 2048
DOM = 32
FEAT = 4
SLOTS = 256
TILE = 128
TILES = 96
LOCAL_TILES = 32
OWN_TILES = NODES // TILE
RECV_TILES = DOM * SLOTS // TILE
HALF = NODES // 2
HALF_TILES = OWN_TILES // 2
LOW = 256
HIGH = NODES // LOW
HUBS = 4096
HID = FEAT * COLS
EARLY = 2 * COLS + COLS // 2

SPARE_TILES = 576
SPARE_SUMS = 288
SPARE_ROWS = 2304
LIST = 1024
LISTS = 4608

SMEM = pl.BlockSpec(memory_space=pltpu.SMEM)
ANY = pl.BlockSpec(memory_space=pl.ANY)


def dot(a, b, dims):
    return lax.dot_general(a, b, dims, preferred_element_type=F32)


def shape(*dims, dtype=BF):
    return jax.ShapeDtypeStruct(dims, dtype)


VMEM = pl.BlockSpec(memory_space=pltpu.VMEM)


def local_call(kernel, outs, args, name, places=(), scratch=(), flops=10**9, size=2**21, mib=14, alias=()):
    places = dict(places)
    return pl.pallas_call(
        kernel,
        out_shape=outs,
        in_specs=[places.get(i, VMEM) for i in range(len(args))],
        out_specs=[places.get(100 + i, SMEM if o.dtype == I32 else VMEM) for i, o in enumerate(outs)],
        scratch_shapes=list(scratch),
        input_output_aliases=dict(alias),
        compiler_params=pltpu.CompilerParams(vmem_limit_bytes=mib * 1024 * 1024),
        cost_estimate=pl.CostEstimate(flops=flops, bytes_accessed=size, transcendentals=0),
        name=name,
    )(*args)


def one_hot(low):
    rows = lax.broadcasted_iota(I32, (LOW, low.shape[1]), 0)
    return jnp.where(rows == low, 1.0, 0.0).astype(BF)


def pack_kernel(x_ref, up_ref, self_ref, neigh_ref, keep_ref, send_ref):
    for k, out in enumerate((keep_ref, send_ref)):
        lanes = pl.ds(pl.multiple_of((chip() ^ k) * HALF, HALF), HALF)
        out[:COLS] = x_ref[:, lanes]
        out[COLS : 2 * COLS] = up_ref[:, lanes]
        for part in range(2):
            half = slice(part * COLS // 2, (part + 1) * COLS // 2)
            out[2 * COLS :, 2 * part * HID : (2 * part + 1) * HID] = self_ref[half]
            out[2 * COLS :, (2 * part + 1) * HID : (2 * part + 2) * HID] = neigh_ref[half]


def pack(x, up, self_weight, neigh_weight):
    return local_call(
        pack_kernel,
        [shape(EARLY, HALF)] * 2,
        [x, up, self_weight, neigh_weight],
        "pack",
        places={},
        flops=0,
        mib=60,
    )


GATHER_STEPS = 4


def gather_kernel(x_ref, slot_ref, hub_ref, out_hbm, out_ref, stacked, sems):
    for b in range(HIGH):
        stacked[b * COLS : (b + 1) * COLS, :] = x_ref[:, b * LOW : (b + 1) * LOW]
    group = DOM // GATHER_STEPS
    copies = []
    for step in range(GATHER_STEPS):
        for r in range(step * group, (step + 1) * group):
            index = slot_ref[r : r + 1, :]
            high = index >> 8
            found = dot(stacked[...], one_hot(index & (LOW - 1)), NN)
            out = jnp.zeros((COLS, SLOTS), F32)
            for b in range(HIGH):
                out = jnp.where(high == b, found[b * COLS : (b + 1) * COLS], out)
            out = out.astype(BF)
            out_ref[r, 0] = out[:, :TILE]
            out_ref[r, 1] = out[:, TILE:]
            out_ref[r, 2] = hub_ref[...]
        part = pl.ds(step * group, group)
        copies.append(pltpu.make_async_copy(out_ref.at[part], out_hbm.at[part], sems.at[step]))
        copies[step].start()
    for copy in copies:
        copy.wait()


def gather_rows(x, slots, hubs):
    return local_call(
        gather_kernel,
        [shape(DOM, 3, COLS, TILE)],
        [x, slots, hubs],
        "gather_rows",
        places={100: ANY},
        scratch=[
            pltpu.VMEM((DOM, 3, COLS, TILE), BF),
            pltpu.VMEM((HIGH * COLS, LOW), BF),
            pltpu.SemaphoreType.DMA((GATHER_STEPS,)),
        ],
        flops=4 * 10**9,
        mib=60,
    )[0]


def prepare_kernel(index_ref, x_ref, tile_hbm, list_hbm, sorted_hbm, total_hbm, list_ref, total_ref, tile_ref, sems):
    copy = pltpu.make_async_copy(tile_hbm, tile_ref, sems.at[0])
    copy.start()
    copy.wait()

    def sort(c, count):
        source = index_ref[1, c]
        own = source < OWN_TILES
        to = jnp.where(own, RECV_TILES + jnp.minimum(count, LOCAL_TILES - 1), source - OWN_TILES)
        list_ref[to] = index_ref[0, c]
        list_ref[TILES + to] = c
        pltpu.make_async_copy(tile_ref.at[c], sorted_hbm.at[to], sems.at[1]).start()
        return count + own.astype(I32)

    lax.fori_loop(0, TILES, sort, jnp.int32(0))
    total_ref[...] = jnp.zeros_like(total_ref)
    group = 8

    @pl.loop(0, LOCAL_TILES // group)
    def _(g):
        products = []
        for k in range(group):
            place = RECV_TILES + g * group + k
            c = list_ref[TILES + place]
            s = jnp.minimum(index_ref[1, c], OWN_TILES - 1)
            list_ref[TILES + place] = s
            lanes = pl.ds(pl.multiple_of(s * TILE, TILE), TILE)
            products.append(dot(tile_ref[c], x_ref[:, lanes], NT))
        for k in range(group):
            d = list_ref[RECV_TILES + g * group + k]
            total_ref[d] = total_ref[d] + products[k]

    outs = [
        pltpu.make_async_copy(total_ref, total_hbm.at[pl.ds(0, OWN_TILES)], sems.at[2]),
        pltpu.make_async_copy(list_ref, list_hbm.at[0], sems.at[3]),
    ]
    for copy in outs:
        copy.start()
    for copy in outs:
        copy.wait()
    pltpu.make_async_copy(tile_ref, sorted_hbm.at[pl.ds(0, TILES)], sems.at[1]).wait()


def prepare(index, x, tiles):
    return local_call(
        prepare_kernel,
        [
            shape(LISTS, LIST, dtype=I32),
            shape(SPARE_TILES, TILE, TILE),
            shape(SPARE_SUMS, TILE, COLS, dtype=F32),
        ],
        [index, x, tiles],
        "prepare",
        places={0: SMEM, 2: ANY, 100: ANY, 101: ANY, 102: ANY},
        scratch=[
            pltpu.SMEM((LIST,), I32),
            pltpu.VMEM((OWN_TILES, TILE, COLS), F32),
            pltpu.VMEM((TILES, TILE, TILE), BF),
            pltpu.SemaphoreType.DMA((4,)),
        ],
        mib=60,
    )


HUB_STEPS = 4
KEEP_EARLY = 2
TILE_STEPS = 4
HALF_ROWS = HALF // HUB_STEPS


def half_rows(half, step):
    return pl.ds(pl.multiple_of(half * HALF + step * HALF_ROWS, HALF_ROWS), HALF_ROWS)


def add_hub_rows(hub_ref, half, step, hubs, total, first_tile):
    tiles = HALF_ROWS // TILE
    part = dot(hub_ref[half_rows(half, step)], hubs[...], NT)
    for k in range(tiles):
        t = first_tile + step * tiles + k
        total[t] = total[t] + part[k * TILE : (k + 1) * TILE]


def forward_send_kernel(list_hbm, recv_ref, tile_hbm, local_hbm, hub_hbm, *rest):
    send_ref, keep_ref, hubs, hub_ref, target_ref, tile_ref, total, sems = rest
    away = 1 - chip()
    firsts = [
        pltpu.make_async_copy(src, dst, sems.at[2 * HUB_STEPS + i])
        for i, (src, dst) in enumerate(
            (
                (list_hbm.at[0], target_ref),
                (local_hbm.at[pl.ds(0, OWN_TILES)], total),
            )
        )
    ]
    group = RECV_TILES // TILE_STEPS
    tile_copies = []
    for i in range(TILE_STEPS):
        part = pl.ds(i * group, group)
        tile_copies.append(
            pltpu.make_async_copy(tile_hbm.at[part], tile_ref.at[part], sems.at[2 * HUB_STEPS + 2 + i])
        )
    copies = []
    for h, half in enumerate((away, chip())):
        for i in range(KEEP_EARLY if h else HUB_STEPS):
            rows = half_rows(half, i)
            copies.append(pltpu.make_async_copy(hub_hbm.at[rows], hub_ref.at[rows], sems.at[h * HUB_STEPS + i]))
    for copy in tile_copies[:1] + firsts + tile_copies[1:] + copies:
        copy.start()
    for q in range(DOM):
        hubs[:, q * TILE : (q + 1) * TILE] = recv_ref[q, 2]
    for step in range(TILE_STEPS):
        first = step * group
        tile_copies[step].wait()
        products = [dot(tile_ref[first + k], recv_ref[first // 2 + k // 2, k % 2], NT) for k in range(group)]
        if step == 0:
            for copy in firsts:
                copy.wait()
        for k, product in enumerate(products):
            d = target_ref[first + k]
            total[d] = total[d] + product

    for step in range(HUB_STEPS):
        copies[step].wait()
        add_hub_rows(hub_ref, away, step, hubs, total, away * HALF_TILES)
    for j in range(HALF_TILES):
        send_ref[:, j * TILE : (j + 1) * TILE] = total[away * HALF_TILES + j].T.astype(BF)
        keep_ref[j] = total[chip() * HALF_TILES + j]
    for copy in copies[HUB_STEPS:]:
        copy.wait()


def forward_send(lists, recv, tiles, local, hub_coef):
    return local_call(
        forward_send_kernel,
        [
            shape(COLS, HALF),
            shape(HALF_TILES, TILE, COLS, dtype=F32),
            shape(COLS, HUBS),
            shape(NODES, HUBS),
        ],
        [lists, recv, tiles, local, hub_coef],
        "forward_send",
        places={0: ANY, 2: ANY, 3: ANY, 4: ANY},
        scratch=[
            pltpu.SMEM((LIST,), I32),
            pltpu.VMEM((RECV_TILES, TILE, TILE), BF),
            pltpu.VMEM((OWN_TILES, TILE, COLS), F32),
            pltpu.SemaphoreType.DMA((2 * HUB_STEPS + 2 + TILE_STEPS,)),
        ],
        flops=2 * 10**9,
        size=2**24,
        mib=34,
    )


def forward_keep_kernel(sum_ref, hubs, _, hub_hbm, keep_ref, hub_ref, total, sems):
    copies = []
    for i in range(KEEP_EARLY, HUB_STEPS):
        rows = half_rows(chip(), i)
        copies.append(pltpu.make_async_copy(hub_hbm.at[rows], hub_ref.at[rows], sems.at[i]))
    for copy in copies:
        copy.start()
    total[...] = sum_ref[...]
    for step in range(HUB_STEPS):
        if step >= KEEP_EARLY:
            copies[step - KEEP_EARLY].wait()
        add_hub_rows(hub_ref, chip(), step, hubs, total, 0)
    for j in range(HALF_TILES):
        keep_ref[:, j * TILE : (j + 1) * TILE] = total[j].T.astype(BF)


def forward_keep(sums, hubs, hub, hub_coef):
    return local_call(
        forward_keep_kernel,
        [shape(COLS, HALF), shape(NODES, HUBS)],
        [sums, hubs, hub, hub_coef],
        "forward_keep",
        places={3: ANY},
        scratch=[pltpu.VMEM(sums.shape, F32), pltpu.SemaphoreType.DMA((HUB_STEPS,))],
        size=2**23,
        mib=28,
        alias={2: 1},
    )


def chip():
    return lax.axis_index("feat") // 2


def rows_of(k):
    return pl.ds(pl.multiple_of((lax.axis_index("feat") ^ k) * COLS, COLS), COLS)


def dense_kernel(*rest):
    aggs, earlies, outs, scratch = rest[:4], rest[4:8], rest[8:14], rest[14:]
    keep_grad, send_grad, grad_ref, self_ref, keep_out, send_out = outs
    agg, x, up, neigh_ref, output = scratch
    for k in range(FEAT):
        rows = rows_of(k)
        agg[rows] = aggs[k][...]
        x[rows] = earlies[k][:COLS]
        up[rows] = earlies[k][COLS : 2 * COLS]
        for part in range(2):
            packed = earlies[k][2 * COLS :, part * 2 * HID : (part + 1) * 2 * HID]
            first = (lax.axis_index("feat") ^ k) * COLS + part * COLS // 2
            half = pl.ds(pl.multiple_of(first, COLS // 2), COLS // 2)
            self_ref[half] = packed[:, :HID]
            neigh_ref[half] = packed[:, HID:]
    pre_act = dot(self_ref[...], x[...], TN) + dot(neigh_ref[...], agg[...], TN)
    fall = jnp.exp(jnp.minimum(pre_act, 0.0))
    output[...] = jnp.where(pre_act > 0, pre_act, fall - 1.0).astype(BF)
    slope = jnp.where(pre_act > 0, 1.0, fall)
    grad_pre = (up[...].astype(F32) * slope).astype(BF)
    grad_ref[...] = grad_pre
    weight = jnp.concatenate([neigh_ref[rows_of(0)], neigh_ref[rows_of(2)]], 0)
    grad_agg = dot(weight, grad_pre, NN).astype(BF)
    keep_grad[...] = grad_agg[:COLS]
    send_grad[...] = grad_agg[COLS:]
    keep_out[...] = output[rows_of(0)]
    send_out[...] = output[rows_of(2)]


def dense(aggs, earlies):
    block = pltpu.VMEM((HID, HALF), BF)
    return local_call(
        dense_kernel,
        [shape(COLS, HALF)] * 2 + [shape(HID, HALF), shape(HID, HID)] + [shape(COLS, HALF)] * 2,
        [*aggs, *earlies],
        "dense",
        places={},
        scratch=[block] * 3 + [pltpu.VMEM((HID, HID), BF), block],
    )


HUB_LANES = HUBS // HUB_STEPS


def hub_part(half, step):
    return pl.ds(pl.multiple_of(half * HALF, HALF), HALF), slice(step * HUB_LANES, (step + 1) * HUB_LANES)


def hub_backward_kernel(grad_ref, self_ref, pre_ref, hub_ref, out_ref, keep_back, send_back):
    weight = jnp.concatenate([self_ref[rows_of(0)], self_ref[rows_of(2)]], 0)
    back = dot(weight, pre_ref[...], NN).astype(BF)
    keep_back[...] = back[:COLS]
    send_back[...] = back[COLS:]
    for step in range(HUB_STEPS):
        rows, lanes = hub_part(chip(), step)
        out_ref[:, lanes] = dot(grad_ref[...], hub_ref[rows, lanes], NN)


def hub_backward(grad, self_weight, grad_pre, hub):
    return local_call(
        hub_backward_kernel,
        [shape(COLS, HUBS, dtype=F32), shape(COLS, HALF), shape(COLS, HALF)],
        [grad, self_weight, grad_pre, hub],
        "hub_backward",
        places={},
        size=2**23,
        mib=20,
    )


def split_tiles(keep_ref, come_ref, grads):
    for k, part in enumerate((keep_ref, come_ref)):
        first = (chip() ^ k) * HALF_TILES
        for j in range(HALF_TILES):
            grads[first + j] = part[:, j * TILE : (j + 1) * TILE]


def backward_kernel(list_hbm, keep_ref, come_ref, terms_ref, tile_hbm, hub_ref, *rest):
    out_hbm, out_ref, target_ref, grads, tile_ref, sems = rest
    group = RECV_TILES // HUB_STEPS
    doms = DOM // HUB_STEPS
    out_copies = []
    list_copy = pltpu.make_async_copy(list_hbm.at[0], target_ref, sems.at[HUB_STEPS])
    list_copy.start()
    copies = []
    for i in range(HUB_STEPS):
        part = pl.ds(i * group, group)
        copies.append(pltpu.make_async_copy(tile_hbm.at[part], tile_ref.at[part], sems.at[i]))
        copies[i].start()
    split_tiles(keep_ref, come_ref, grads)
    list_copy.wait()
    for step in range(HUB_STEPS):
        rows, lanes = hub_part(1 - chip(), step)
        terms = (terms_ref[:, lanes] + dot(come_ref[...], hub_ref[rows, lanes], NN)).astype(BF)
        for k in range(doms):
            out_ref[step * doms + k, 2] = terms[:, k * TILE : (k + 1) * TILE]
        copies[step].wait()
        for s in range(step * group, (step + 1) * group):
            out_ref[s // 2, s % 2] = dot(grads[target_ref[s]], tile_ref[s], NN).astype(BF)
        part = pl.ds(step * doms, doms)
        out_copies.append(pltpu.make_async_copy(out_ref.at[part], out_hbm.at[part], sems.at[HUB_STEPS + 1 + step]))
        out_copies[step].start()
    for copy in out_copies:
        copy.wait()


def backward(lists, keep, come, terms, tiles, hub):
    return local_call(
        backward_kernel,
        [shape(DOM, 3, COLS, TILE)],
        [lists, keep, come, terms, tiles, hub],
        "backward",
        places={0: ANY, 4: ANY, 100: ANY},
        scratch=[
            pltpu.VMEM((DOM, 3, COLS, TILE), BF),
            pltpu.SMEM((LIST,), I32),
            pltpu.VMEM((OWN_TILES, COLS, TILE), BF),
            pltpu.VMEM((RECV_TILES, TILE, TILE), BF),
            pltpu.SemaphoreType.DMA((2 * HUB_STEPS + 1,)),
        ],
        flops=2 * 10**9,
        size=2**23,
        mib=20,
    )[0]


def own_backward_kernel(list_hbm, keep_ref, come_ref, tile_hbm, own_hbm, *rest):
    list_ref, own_ref, grads, total, tile_ref, sems = rest
    copies = [
        pltpu.make_async_copy(list_hbm.at[0], list_ref, sems.at[0]),
        pltpu.make_async_copy(tile_hbm.at[pl.ds(RECV_TILES, LOCAL_TILES)], tile_ref, sems.at[1]),
    ]
    for copy in copies:
        copy.start()
    split_tiles(keep_ref, come_ref, grads)
    total[...] = jnp.zeros_like(total)
    for copy in copies:
        copy.wait()
    group = 8

    @pl.loop(0, LOCAL_TILES // group)
    def _(g):
        places = [RECV_TILES + g * group + k for k in range(group)]
        products = [dot(grads[list_ref[c]], tile_ref[c - RECV_TILES], NN) for c in places]
        for c, product in zip(places, products):
            s = list_ref[TILES + c]
            total[s] = total[s] + product

    for t in range(OWN_TILES):
        own_ref[:, t * TILE : (t + 1) * TILE] = total[t]
    out_copy = pltpu.make_async_copy(own_ref, own_hbm.at[pl.ds(0, COLS)], sems.at[2])
    out_copy.start()
    out_copy.wait()


def own_backward(lists, keep, come, tiles):
    return local_call(
        own_backward_kernel,
        [shape(SPARE_ROWS, NODES, dtype=F32)],
        [lists, keep, come, tiles],
        "own_backward",
        places={0: ANY, 3: ANY, 100: ANY},
        scratch=[
            pltpu.SMEM((LIST,), I32),
            pltpu.VMEM((COLS, NODES), F32),
            pltpu.VMEM((OWN_TILES, COLS, TILE), BF),
            pltpu.VMEM((OWN_TILES, COLS, TILE), F32),
            pltpu.VMEM((LOCAL_TILES, TILE, TILE), BF),
            pltpu.SemaphoreType.DMA((3,)),
        ],
        mib=60,
    )[0]


def scatter_kernel(slot_ref, recv_ref, own_hbm, keep_ref, come_ref, out_keep, out_come, *rest):
    grad_ref, hub_ref, output_ref, total, own_ref, sems = rest
    own_copy = pltpu.make_async_copy(own_hbm.at[pl.ds(0, COLS)], own_ref, sems.at[0])
    own_copy.start()
    total[...] = jnp.zeros_like(total)
    group = 16

    @pl.loop(0, DOM // group)
    def _(g):
        spread, hots = [], []
        for k in range(group):
            r = g * group + k
            index = slot_ref[pl.ds(r, 1), :]
            high = index >> 8
            rows = jnp.concatenate([recv_ref[r, 0], recv_ref[r, 1]], 1)
            spread.append(
                jnp.concatenate([jnp.where(high == b, rows, jnp.zeros_like(rows)) for b in range(HIGH)], 0)
            )
            hots.append(one_hot(index & (LOW - 1)))
        total[...] += dot(jnp.concatenate(spread, 1), jnp.concatenate(hots, 1), NT)

    hub = jnp.zeros((COLS, TILE), F32)
    for r in range(DOM):
        hub = hub + recv_ref[r, 2].astype(F32)
    hub_ref[...] = hub
    own_copy.wait()
    for b in range(HIGH):
        lanes = slice(b * LOW, (b + 1) * LOW)
        grad_ref[:, lanes] = total[b * COLS : (b + 1) * COLS] + own_ref[:, lanes]
    keep = pl.ds(pl.multiple_of(chip() * HALF, HALF), HALF)
    come = pl.ds(pl.multiple_of((1 - chip()) * HALF, HALF), HALF)
    grad_ref[:, keep] = grad_ref[:, keep] + keep_ref[...].astype(F32)
    grad_ref[:, come] = grad_ref[:, come] + come_ref[...].astype(F32)
    output_ref[:, keep] = out_keep[...]
    output_ref[:, come] = out_come[...]


def scatter_rows(slots, recv, own, keep, come, out_keep, out_come):
    return local_call(
        scatter_kernel,
        [shape(COLS, NODES, dtype=F32), shape(COLS, TILE, dtype=F32), shape(COLS, NODES)],
        [slots, recv, own, keep, come, out_keep, out_come],
        "scatter_rows",
        places={2: ANY},
        scratch=[
            pltpu.VMEM((HIGH * COLS, LOW), F32),
            pltpu.VMEM((COLS, NODES), F32),
            pltpu.SemaphoreType.DMA((1,)),
        ],
        mib=47,
    )


def to_dom(x):
    return lax.all_to_all(x, "dom", split_axis=0, concat_axis=0, tiled=True)


def swap(x, k):
    return lax.ppermute(x, "feat", [(f, f ^ k) for f in range(FEAT)])


def after(x, *others):
    return lax.optimization_barrier((x, *others))[0]


def body(
    features,
    hub_feats,
    hub_coef,
    tile_coef,
    tile_index,
    boundary_rows,
    self_weight,
    neigh_weight,
    out_grad,
):
    x = features.T
    up = out_grad.T
    slots = boundary_rows[0]
    index = tile_index.T

    outgoing = gather_rows(x, slots, hub_feats.T)
    incoming = to_dom(outgoing)
    x_in, up_in = lax.optimization_barrier((x, up, outgoing))[:2]
    early, early_send = pack(x_in, up_in, self_weight, neigh_weight)
    early_2 = swap(early_send, 2)
    early_1 = swap(early, 1)
    lists, tiles, local_sum = prepare(index, x_in, tile_coef)
    agg_send, sums, hubs, hub = forward_send(lists, incoming, tiles, local_sum, hub_coef)
    agg_2 = swap(agg_send, 2)
    early_2 = after(early_2, agg_send)
    early = [early, early_1, early_2, swap(early_2, 1)]
    agg, hub = forward_keep(sums, hubs, hub, hub_coef)
    grad, grad_send, grad_pre, self_weight, out_keep, out_send = dense(
        [agg, swap(agg, 1), agg_2, swap(agg_2, 1)], early
    )
    grad_2 = swap(grad_send, 2)
    terms, back, back_send = hub_backward(grad, self_weight, grad_pre, hub)
    back_2 = swap(back_send, 2)
    sums = backward(lists, grad, grad_2, terms, tiles, hub)
    sums, back_2, out_send = lax.optimization_barrier((sums, back_2, out_send))
    returned = to_dom(sums)
    out_2 = swap(out_send, 2)
    own_grad = own_backward(lists, after(grad, sums), grad_2, tiles)
    grad_feats, grad_hubs, output_rows = scatter_rows(
        slots, returned, own_grad, back, back_2, out_keep, out_2
    )
    return (output_rows.T, grad_feats.T, grad_hubs.T)


def solution(mesh):
    return jax.shard_map(
        body,
        mesh=mesh,
        in_specs=(
            P("dom", "feat"),
            P("dom", "feat"),
            P("dom", None),
            P("dom", None, None),
            P("dom", None),
            P("dom", None, None),
            P("feat", None),
            P("feat", None),
            P("dom", "feat"),
        ),
        out_specs=(P("dom", "feat"), P("dom", "feat"), P("dom", "feat")),
        check_vma=False,
    )
```

```python
import jax
import jax.numpy as jnp
from jax import lax
from jax.experimental import pallas as pl
from jax.experimental.pallas import tpu as pltpu
from jax.sharding import PartitionSpec as P

BF = jnp.bfloat16
F32 = jnp.float32
I32 = jnp.int32
NT = (((1,), (1,)), ((), ()))
NN = (((1,), (0,)), ((), ()))
TN = (((0,), (0,)), ((), ()))

COLS = 64
NODES = 2048
DOM = 32
FEAT = 4
SLOTS = 256
TILE = 128
TILES = 96
LOCAL_TILES = 32
OWN_TILES = NODES // TILE
RECV_TILES = DOM * SLOTS // TILE
HALF = NODES // 2
HALF_TILES = OWN_TILES // 2
LOW = 256
HIGH = NODES // LOW
HUBS = 4096
HID = FEAT * COLS
EARLY = 2 * COLS + COLS // 2

SPARE_TILES = 576
SPARE_SUMS = 288
SPARE_ROWS = 2304
LIST = 1024
LISTS = 4608

SMEM = pl.BlockSpec(memory_space=pltpu.SMEM)
ANY = pl.BlockSpec(memory_space=pl.ANY)


def dot(a, b, dims):
    return lax.dot_general(a, b, dims, preferred_element_type=F32)


def shape(*dims, dtype=BF):
    return jax.ShapeDtypeStruct(dims, dtype)


VMEM = pl.BlockSpec(memory_space=pltpu.VMEM)


def local_call(kernel, outs, args, name, places=(), scratch=(), flops=10**9, size=2**21, mib=14, alias=()):
    places = dict(places)
    return pl.pallas_call(
        kernel,
        out_shape=outs,
        in_specs=[places.get(i, VMEM) for i in range(len(args))],
        out_specs=[places.get(100 + i, SMEM if o.dtype == I32 else VMEM) for i, o in enumerate(outs)],
        scratch_shapes=list(scratch),
        input_output_aliases=dict(alias),
        compiler_params=pltpu.CompilerParams(vmem_limit_bytes=mib * 1024 * 1024),
        cost_estimate=pl.CostEstimate(flops=flops, bytes_accessed=size, transcendentals=0),
        name=name,
    )(*args)


def one_hot(low):
    rows = lax.broadcasted_iota(I32, (LOW, low.shape[1]), 0)
    return jnp.where(rows == low, 1.0, 0.0).astype(BF)


def pack_kernel(x_ref, up_ref, self_ref, neigh_ref, keep_ref, send_ref):
    for k, out in enumerate((keep_ref, send_ref)):
        lanes = pl.ds(pl.multiple_of((chip() ^ k) * HALF, HALF), HALF)
        out[:COLS] = x_ref[:, lanes]
        out[COLS : 2 * COLS] = up_ref[:, lanes]
        for part in range(2):
            half = slice(part * COLS // 2, (part + 1) * COLS // 2)
            out[2 * COLS :, 2 * part * HID : (2 * part + 1) * HID] = self_ref[half]
            out[2 * COLS :, (2 * part + 1) * HID : (2 * part + 2) * HID] = neigh_ref[half]


def pack(x, up, self_weight, neigh_weight):
    return local_call(
        pack_kernel,
        [shape(EARLY, HALF)] * 2,
        [x, up, self_weight, neigh_weight],
        "pack",
        places={},
        flops=0,
        mib=60,
    )


GATHER_STEPS = 4


def gather_kernel(x_ref, slot_ref, hub_ref, out_hbm, out_ref, stacked, sems):
    for b in range(HIGH):
        stacked[b * COLS : (b + 1) * COLS, :] = x_ref[:, b * LOW : (b + 1) * LOW]
    group = DOM // GATHER_STEPS
    copies = []
    for step in range(GATHER_STEPS):
        for r in range(step * group, (step + 1) * group):
            index = slot_ref[r : r + 1, :]
            high = index >> 8
            found = dot(stacked[...], one_hot(index & (LOW - 1)), NN)
            out = jnp.zeros((COLS, SLOTS), F32)
            for b in range(HIGH):
                out = jnp.where(high == b, found[b * COLS : (b + 1) * COLS], out)
            out = out.astype(BF)
            out_ref[r, 0] = out[:, :TILE]
            out_ref[r, 1] = out[:, TILE:]
            out_ref[r, 2] = hub_ref[...]
        part = pl.ds(step * group, group)
        copies.append(pltpu.make_async_copy(out_ref.at[part], out_hbm.at[part], sems.at[step]))
        copies[step].start()
    for copy in copies:
        copy.wait()


def gather_rows(x, slots, hubs):
    return local_call(
        gather_kernel,
        [shape(DOM, 3, COLS, TILE)],
        [x, slots, hubs],
        "gather_rows",
        places={100: ANY},
        scratch=[
            pltpu.VMEM((DOM, 3, COLS, TILE), BF),
            pltpu.VMEM((HIGH * COLS, LOW), BF),
            pltpu.SemaphoreType.DMA((GATHER_STEPS,)),
        ],
        flops=4 * 10**9,
        mib=60,
    )[0]


def prepare_kernel(index_ref, x_ref, tile_hbm, list_hbm, sorted_hbm, total_hbm, list_ref, total_ref, tile_ref, sems):
    copy = pltpu.make_async_copy(tile_hbm, tile_ref, sems.at[0])
    copy.start()
    copy.wait()

    def sort(c, count):
        source = index_ref[1, c]
        own = source < OWN_TILES
        to = jnp.where(own, RECV_TILES + jnp.minimum(count, LOCAL_TILES - 1), source - OWN_TILES)
        list_ref[to] = index_ref[0, c]
        list_ref[TILES + to] = c
        pltpu.make_async_copy(tile_ref.at[c], sorted_hbm.at[to], sems.at[1]).start()
        return count + own.astype(I32)

    lax.fori_loop(0, TILES, sort, jnp.int32(0))
    total_ref[...] = jnp.zeros_like(total_ref)
    group = 8

    @pl.loop(0, LOCAL_TILES // group)
    def _(g):
        products = []
        for k in range(group):
            place = RECV_TILES + g * group + k
            c = list_ref[TILES + place]
            s = jnp.minimum(index_ref[1, c], OWN_TILES - 1)
            list_ref[TILES + place] = s
            lanes = pl.ds(pl.multiple_of(s * TILE, TILE), TILE)
            products.append(dot(tile_ref[c], x_ref[:, lanes], NT))
        for k in range(group):
            d = list_ref[RECV_TILES + g * group + k]
            total_ref[d] = total_ref[d] + products[k]

    outs = [
        pltpu.make_async_copy(total_ref, total_hbm.at[pl.ds(0, OWN_TILES)], sems.at[2]),
        pltpu.make_async_copy(list_ref, list_hbm.at[0], sems.at[3]),
    ]
    for copy in outs:
        copy.start()
    for copy in outs:
        copy.wait()
    pltpu.make_async_copy(tile_ref, sorted_hbm.at[pl.ds(0, TILES)], sems.at[1]).wait()


def prepare(index, x, tiles):
    return local_call(
        prepare_kernel,
        [
            shape(LISTS, LIST, dtype=I32),
            shape(SPARE_TILES, TILE, TILE),
            shape(SPARE_SUMS, TILE, COLS, dtype=F32),
        ],
        [index, x, tiles],
        "prepare",
        places={0: SMEM, 2: ANY, 100: ANY, 101: ANY, 102: ANY},
        scratch=[
            pltpu.SMEM((LIST,), I32),
            pltpu.VMEM((OWN_TILES, TILE, COLS), F32),
            pltpu.VMEM((TILES, TILE, TILE), BF),
            pltpu.SemaphoreType.DMA((4,)),
        ],
        mib=60,
    )


HUB_STEPS = 4
KEEP_EARLY = 2
TILE_STEPS = 4
HALF_ROWS = HALF // HUB_STEPS


def half_rows(half, step):
    return pl.ds(pl.multiple_of(half * HALF + step * HALF_ROWS, HALF_ROWS), HALF_ROWS)


def add_hub_rows(hub_ref, half, step, hubs, total, first_tile):
    tiles = HALF_ROWS // TILE
    part = dot(hub_ref[half_rows(half, step)], hubs[...], NT)
    for k in range(tiles):
        t = first_tile + step * tiles + k
        total[t] = total[t] + part[k * TILE : (k + 1) * TILE]


def forward_send_kernel(list_hbm, recv_ref, tile_hbm, local_hbm, hub_hbm, *rest):
    send_ref, keep_ref, hubs, hub_ref, target_ref, tile_ref, total, sems = rest
    away = 1 - chip()
    firsts = [
        pltpu.make_async_copy(src, dst, sems.at[2 * HUB_STEPS + i])
        for i, (src, dst) in enumerate(
            (
                (list_hbm.at[0], target_ref),
                (local_hbm.at[pl.ds(0, OWN_TILES)], total),
            )
        )
    ]
    group = RECV_TILES // TILE_STEPS
    tile_copies = []
    for i in range(TILE_STEPS):
        part = pl.ds(i * group, group)
        tile_copies.append(
            pltpu.make_async_copy(tile_hbm.at[part], tile_ref.at[part], sems.at[2 * HUB_STEPS + 2 + i])
        )
    copies = []
    for h, half in enumerate((away, chip())):
        for i in range(KEEP_EARLY if h else HUB_STEPS):
            rows = half_rows(half, i)
            copies.append(pltpu.make_async_copy(hub_hbm.at[rows], hub_ref.at[rows], sems.at[h * HUB_STEPS + i]))
    for copy in tile_copies[:1] + firsts + tile_copies[1:] + copies:
        copy.start()
    for q in range(DOM):
        hubs[:, q * TILE : (q + 1) * TILE] = recv_ref[q, 2]
    for step in range(TILE_STEPS):
        first = step * group
        tile_copies[step].wait()
        products = [dot(tile_ref[first + k], recv_ref[first // 2 + k // 2, k % 2], NT) for k in range(group)]
        if step == 0:
            for copy in firsts:
                copy.wait()
        for k, product in enumerate(products):
            d = target_ref[first + k]
            total[d] = total[d] + product

    for step in range(HUB_STEPS):
        copies[step].wait()
        add_hub_rows(hub_ref, away, step, hubs, total, away * HALF_TILES)
    for j in range(HALF_TILES):
        send_ref[:, j * TILE : (j + 1) * TILE] = total[away * HALF_TILES + j].T.astype(BF)
        keep_ref[j] = total[chip() * HALF_TILES + j]
    for copy in copies[HUB_STEPS:]:
        copy.wait()


def forward_send(lists, recv, tiles, local, hub_coef):
    return local_call(
        forward_send_kernel,
        [
            shape(COLS, HALF),
            shape(HALF_TILES, TILE, COLS, dtype=F32),
            shape(COLS, HUBS),
            shape(NODES, HUBS),
        ],
        [lists, recv, tiles, local, hub_coef],
        "forward_send",
        places={0: ANY, 2: ANY, 3: ANY, 4: ANY},
        scratch=[
            pltpu.SMEM((LIST,), I32),
            pltpu.VMEM((RECV_TILES, TILE, TILE), BF),
            pltpu.VMEM((OWN_TILES, TILE, COLS), F32),
            pltpu.SemaphoreType.DMA((2 * HUB_STEPS + 2 + TILE_STEPS,)),
        ],
        flops=2 * 10**9,
        size=2**24,
        mib=34,
    )


def forward_keep_kernel(sum_ref, hubs, _, hub_hbm, keep_ref, hub_ref, total, sems):
    copies = []
    for i in range(KEEP_EARLY, HUB_STEPS):
        rows = half_rows(chip(), i)
        copies.append(pltpu.make_async_copy(hub_hbm.at[rows], hub_ref.at[rows], sems.at[i]))
    for copy in copies:
        copy.start()
    total[...] = sum_ref[...]
    for step in range(HUB_STEPS):
        if step >= KEEP_EARLY:
            copies[step - KEEP_EARLY].wait()
        add_hub_rows(hub_ref, chip(), step, hubs, total, 0)
    for j in range(HALF_TILES):
        keep_ref[:, j * TILE : (j + 1) * TILE] = total[j].T.astype(BF)


def forward_keep(sums, hubs, hub, hub_coef):
    return local_call(
        forward_keep_kernel,
        [shape(COLS, HALF), shape(NODES, HUBS)],
        [sums, hubs, hub, hub_coef],
        "forward_keep",
        places={3: ANY},
        scratch=[pltpu.VMEM(sums.shape, F32), pltpu.SemaphoreType.DMA((HUB_STEPS,))],
        size=2**23,
        mib=28,
        alias={2: 1},
    )


def chip():
    return lax.axis_index("feat") // 2


def rows_of(k):
    return pl.ds(pl.multiple_of((lax.axis_index("feat") ^ k) * COLS, COLS), COLS)


def dense_kernel(*rest):
    aggs, earlies, outs, scratch = rest[:4], rest[4:8], rest[8:14], rest[14:]
    keep_grad, send_grad, grad_ref, self_ref, keep_out, send_out = outs
    agg, x, up, neigh_ref, output = scratch
    for k in range(FEAT):
        rows = rows_of(k)
        agg[rows] = aggs[k][...]
        x[rows] = earlies[k][:COLS]
        up[rows] = earlies[k][COLS : 2 * COLS]
        for part in range(2):
            packed = earlies[k][2 * COLS :, part * 2 * HID : (part + 1) * 2 * HID]
            first = (lax.axis_index("feat") ^ k) * COLS + part * COLS // 2
            half = pl.ds(pl.multiple_of(first, COLS // 2), COLS // 2)
            self_ref[half] = packed[:, :HID]
            neigh_ref[half] = packed[:, HID:]
    pre_act = dot(self_ref[...], x[...], TN) + dot(neigh_ref[...], agg[...], TN)
    fall = jnp.exp(jnp.minimum(pre_act, 0.0))
    output[...] = jnp.where(pre_act > 0, pre_act, fall - 1.0).astype(BF)
    slope = jnp.where(pre_act > 0, 1.0, fall)
    grad_pre = (up[...].astype(F32) * slope).astype(BF)
    grad_ref[...] = grad_pre
    weight = jnp.concatenate([neigh_ref[rows_of(0)], neigh_ref[rows_of(2)]], 0)
    grad_agg = dot(weight, grad_pre, NN).astype(BF)
    keep_grad[...] = grad_agg[:COLS]
    send_grad[...] = grad_agg[COLS:]
    keep_out[...] = output[rows_of(0)]
    send_out[...] = output[rows_of(2)]


def dense(aggs, earlies):
    block = pltpu.VMEM((HID, HALF), BF)
    return local_call(
        dense_kernel,
        [shape(COLS, HALF)] * 2 + [shape(HID, HALF), shape(HID, HID)] + [shape(COLS, HALF)] * 2,
        [*aggs, *earlies],
        "dense",
        places={},
        scratch=[block] * 3 + [pltpu.VMEM((HID, HID), BF), block],
    )


HUB_LANES = HUBS // HUB_STEPS


def hub_part(half, step):
    return pl.ds(pl.multiple_of(half * HALF, HALF), HALF), slice(step * HUB_LANES, (step + 1) * HUB_LANES)


def hub_backward_kernel(grad_ref, self_ref, pre_ref, hub_ref, out_ref, keep_back, send_back):
    weight = jnp.concatenate([self_ref[rows_of(0)], self_ref[rows_of(2)]], 0)
    back = dot(weight, pre_ref[...], NN).astype(BF)
    keep_back[...] = back[:COLS]
    send_back[...] = back[COLS:]
    for step in range(HUB_STEPS):
        rows, lanes = hub_part(chip(), step)
        out_ref[:, lanes] = dot(grad_ref[...], hub_ref[rows, lanes], NN)


def hub_backward(grad, self_weight, grad_pre, hub):
    return local_call(
        hub_backward_kernel,
        [shape(COLS, HUBS, dtype=F32), shape(COLS, HALF), shape(COLS, HALF)],
        [grad, self_weight, grad_pre, hub],
        "hub_backward",
        places={},
        size=2**23,
        mib=20,
    )


def split_tiles(keep_ref, come_ref, grads):
    for k, part in enumerate((keep_ref, come_ref)):
        first = (chip() ^ k) * HALF_TILES
        for j in range(HALF_TILES):
            grads[first + j] = part[:, j * TILE : (j + 1) * TILE]


def backward_kernel(list_hbm, keep_ref, come_ref, terms_ref, tile_hbm, hub_ref, *rest):
    out_hbm, out_ref, target_ref, grads, tile_ref, sems = rest
    group = RECV_TILES // HUB_STEPS
    doms = DOM // HUB_STEPS
    out_copies = []
    list_copy = pltpu.make_async_copy(list_hbm.at[0], target_ref, sems.at[HUB_STEPS])
    list_copy.start()
    copies = []
    for i in range(HUB_STEPS):
        part = pl.ds(i * group, group)
        copies.append(pltpu.make_async_copy(tile_hbm.at[part], tile_ref.at[part], sems.at[i]))
        copies[i].start()
    split_tiles(keep_ref, come_ref, grads)
    list_copy.wait()
    for step in range(HUB_STEPS):
        rows, lanes = hub_part(1 - chip(), step)
        terms = (terms_ref[:, lanes] + dot(come_ref[...], hub_ref[rows, lanes], NN)).astype(BF)
        for k in range(doms):
            out_ref[step * doms + k, 2] = terms[:, k * TILE : (k + 1) * TILE]
        copies[step].wait()
        for s in range(step * group, (step + 1) * group):
            out_ref[s // 2, s % 2] = dot(grads[target_ref[s]], tile_ref[s], NN).astype(BF)
        part = pl.ds(step * doms, doms)
        out_copies.append(pltpu.make_async_copy(out_ref.at[part], out_hbm.at[part], sems.at[HUB_STEPS + 1 + step]))
        out_copies[step].start()
    for copy in out_copies:
        copy.wait()


def backward(lists, keep, come, terms, tiles, hub):
    return local_call(
        backward_kernel,
        [shape(DOM, 3, COLS, TILE)],
        [lists, keep, come, terms, tiles, hub],
        "backward",
        places={0: ANY, 4: ANY, 100: ANY},
        scratch=[
            pltpu.VMEM((DOM, 3, COLS, TILE), BF),
            pltpu.SMEM((LIST,), I32),
            pltpu.VMEM((OWN_TILES, COLS, TILE), BF),
            pltpu.VMEM((RECV_TILES, TILE, TILE), BF),
            pltpu.SemaphoreType.DMA((2 * HUB_STEPS + 1,)),
        ],
        flops=2 * 10**9,
        size=2**23,
        mib=20,
    )[0]


def own_backward_kernel(list_hbm, keep_ref, come_ref, tile_hbm, own_hbm, *rest):
    list_ref, own_ref, grads, total, tile_ref, sems = rest
    copies = [
        pltpu.make_async_copy(list_hbm.at[0], list_ref, sems.at[0]),
        pltpu.make_async_copy(tile_hbm.at[pl.ds(RECV_TILES, LOCAL_TILES)], tile_ref, sems.at[1]),
    ]
    for copy in copies:
        copy.start()
    split_tiles(keep_ref, come_ref, grads)
    total[...] = jnp.zeros_like(total)
    for copy in copies:
        copy.wait()
    group = 8

    @pl.loop(0, LOCAL_TILES // group)
    def _(g):
        places = [RECV_TILES + g * group + k for k in range(group)]
        products = [dot(grads[list_ref[c]], tile_ref[c - RECV_TILES], NN) for c in places]
        for c, product in zip(places, products):
            s = list_ref[TILES + c]
            total[s] = total[s] + product

    for t in range(OWN_TILES):
        own_ref[:, t * TILE : (t + 1) * TILE] = total[t]
    out_copy = pltpu.make_async_copy(own_ref, own_hbm.at[pl.ds(0, COLS)], sems.at[2])
    out_copy.start()
    out_copy.wait()


def own_backward(lists, keep, come, tiles):
    return local_call(
        own_backward_kernel,
        [shape(SPARE_ROWS, NODES, dtype=F32)],
        [lists, keep, come, tiles],
        "own_backward",
        places={0: ANY, 3: ANY, 100: ANY},
        scratch=[
            pltpu.SMEM((LIST,), I32),
            pltpu.VMEM((COLS, NODES), F32),
            pltpu.VMEM((OWN_TILES, COLS, TILE), BF),
            pltpu.VMEM((OWN_TILES, COLS, TILE), F32),
            pltpu.VMEM((LOCAL_TILES, TILE, TILE), BF),
            pltpu.SemaphoreType.DMA((3,)),
        ],
        mib=60,
    )[0]


def scatter_kernel(slot_ref, recv_ref, own_hbm, keep_ref, come_ref, out_keep, out_come, *rest):
    grad_ref, hub_ref, output_ref, total, own_ref, sems = rest
    own_copy = pltpu.make_async_copy(own_hbm.at[pl.ds(0, COLS)], own_ref, sems.at[0])
    own_copy.start()
    total[...] = jnp.zeros_like(total)
    group = 16

    @pl.loop(0, DOM // group)
    def _(g):
        spread, hots = [], []
        for k in range(group):
            r = g * group + k
            index = slot_ref[pl.ds(r, 1), :]
            high = index >> 8
            rows = jnp.concatenate([recv_ref[r, 0], recv_ref[r, 1]], 1)
            spread.append(
                jnp.concatenate([jnp.where(high == b, rows, jnp.zeros_like(rows)) for b in range(HIGH)], 0)
            )
            hots.append(one_hot(index & (LOW - 1)))
        total[...] += dot(jnp.concatenate(spread, 1), jnp.concatenate(hots, 1), NT)

    hub = jnp.zeros((COLS, TILE), F32)
    for r in range(DOM):
        hub = hub + recv_ref[r, 2].astype(F32)
    hub_ref[...] = hub
    own_copy.wait()
    for b in range(HIGH):
        lanes = slice(b * LOW, (b + 1) * LOW)
        grad_ref[:, lanes] = total[b * COLS : (b + 1) * COLS] + own_ref[:, lanes]
    keep = pl.ds(pl.multiple_of(chip() * HALF, HALF), HALF)
    come = pl.ds(pl.multiple_of((1 - chip()) * HALF, HALF), HALF)
    grad_ref[:, keep] = grad_ref[:, keep] + keep_ref[...].astype(F32)
    grad_ref[:, come] = grad_ref[:, come] + come_ref[...].astype(F32)
    output_ref[:, keep] = out_keep[...]
    output_ref[:, come] = out_come[...]


def scatter_rows(slots, recv, own, keep, come, out_keep, out_come):
    return local_call(
        scatter_kernel,
        [shape(COLS, NODES, dtype=F32), shape(COLS, TILE, dtype=F32), shape(COLS, NODES)],
        [slots, recv, own, keep, come, out_keep, out_come],
        "scatter_rows",
        places={2: ANY},
        scratch=[
            pltpu.VMEM((HIGH * COLS, LOW), F32),
            pltpu.VMEM((COLS, NODES), F32),
            pltpu.SemaphoreType.DMA((1,)),
        ],
        mib=47,
    )


def to_dom(x):
    return lax.all_to_all(x, "dom", split_axis=0, concat_axis=0, tiled=True)


def swap(x, k):
    return lax.ppermute(x, "feat", [(f, f ^ k) for f in range(FEAT)])


def after(x, *others):
    return lax.optimization_barrier((x, *others))[0]


def body(
    features,
    hub_feats,
    hub_coef,
    tile_coef,
    tile_index,
    boundary_rows,
    self_weight,
    neigh_weight,
    out_grad,
):
    x = features.T
    up = out_grad.T
    slots = boundary_rows[0]
    index = tile_index.T

    outgoing = gather_rows(x, slots, hub_feats.T)
    incoming = to_dom(outgoing)
    x_in, up_in = lax.optimization_barrier((x, up, outgoing))[:2]
    early, early_send = pack(x_in, up_in, self_weight, neigh_weight)
    early_2 = swap(early_send, 2)
    early_1 = swap(early, 1)
    lists, tiles, local_sum = prepare(index, x_in, tile_coef)
    agg_send, sums, hubs, hub = forward_send(lists, incoming, tiles, local_sum, hub_coef)
    agg_2 = swap(agg_send, 2)
    agg, hub = forward_keep(sums, hubs, hub, hub_coef)
    early_2, agg_2, agg = lax.optimization_barrier((early_2, agg_2, agg))
    early = [early, early_1, early_2, swap(early_2, 1)]
    grad, grad_send, grad_pre, self_weight, out_keep, out_send = dense(
        [agg, swap(agg, 1), agg_2, swap(agg_2, 1)], early
    )
    grad_2 = swap(grad_send, 2)
    terms, back, back_send = hub_backward(grad, self_weight, grad_pre, hub)
    back_2 = swap(back_send, 2)
    sums = backward(lists, grad, grad_2, terms, tiles, hub)
    sums, back_2, out_send = lax.optimization_barrier((sums, back_2, out_send))
    returned = to_dom(sums)
    out_2 = swap(out_send, 2)
    own_grad = own_backward(lists, after(grad, sums), grad_2, tiles)
    grad_feats, grad_hubs, output_rows = scatter_rows(
        slots, returned, own_grad, back, back_2, out_keep, out_2
    )
    return (output_rows.T, grad_feats.T, grad_hubs.T)


def solution(mesh):
    return jax.shard_map(
        body,
        mesh=mesh,
        in_specs=(
            P("dom", "feat"),
            P("dom", "feat"),
            P("dom", None),
            P("dom", None, None),
            P("dom", None),
            P("dom", None, None),
            P("feat", None),
            P("feat", None),
            P("dom", "feat"),
        ),
        out_specs=(P("dom", "feat"), P("dom", "feat"), P("dom", "feat")),
        check_vma=False,
    )
```

```python
import jax
import jax.numpy as jnp
from jax import lax
from jax.experimental import pallas as pl
from jax.experimental.pallas import tpu as pltpu
from jax.sharding import PartitionSpec as P

BF = jnp.bfloat16
F32 = jnp.float32
I32 = jnp.int32
NT = (((1,), (1,)), ((), ()))
NN = (((1,), (0,)), ((), ()))
TN = (((0,), (0,)), ((), ()))

COLS = 64
NODES = 2048
DOM = 32
FEAT = 4
SLOTS = 256
TILE = 128
TILES = 96
LOCAL_TILES = 32
OWN_TILES = NODES // TILE
RECV_TILES = DOM * SLOTS // TILE
HALF = NODES // 2
HALF_TILES = OWN_TILES // 2
LOW = 256
HIGH = NODES // LOW
HUBS = 4096
HID = FEAT * COLS
EARLY = 2 * COLS + COLS // 2

SPARE_TILES = 576
SPARE_SUMS = 288
SPARE_ROWS = 2304
LIST = 1024
LISTS = 4608

SMEM = pl.BlockSpec(memory_space=pltpu.SMEM)
ANY = pl.BlockSpec(memory_space=pl.ANY)


def dot(a, b, dims):
    return lax.dot_general(a, b, dims, preferred_element_type=F32)


def shape(*dims, dtype=BF):
    return jax.ShapeDtypeStruct(dims, dtype)


VMEM = pl.BlockSpec(memory_space=pltpu.VMEM)


def local_call(kernel, outs, args, name, places=(), scratch=(), flops=10**9, size=2**21, mib=14, alias=()):
    places = dict(places)
    return pl.pallas_call(
        kernel,
        out_shape=outs,
        in_specs=[places.get(i, VMEM) for i in range(len(args))],
        out_specs=[places.get(100 + i, SMEM if o.dtype == I32 else VMEM) for i, o in enumerate(outs)],
        scratch_shapes=list(scratch),
        input_output_aliases=dict(alias),
        compiler_params=pltpu.CompilerParams(vmem_limit_bytes=mib * 1024 * 1024),
        cost_estimate=pl.CostEstimate(flops=flops, bytes_accessed=size, transcendentals=0),
        name=name,
    )(*args)


def one_hot(low):
    rows = lax.broadcasted_iota(I32, (LOW, low.shape[1]), 0)
    return jnp.where(rows == low, 1.0, 0.0).astype(BF)


def pack_kernel(x_ref, up_ref, self_ref, neigh_ref, keep_ref, send_ref):
    for k, out in enumerate((keep_ref, send_ref)):
        lanes = pl.ds(pl.multiple_of((chip() ^ k) * HALF, HALF), HALF)
        out[:COLS] = x_ref[:, lanes]
        out[COLS : 2 * COLS] = up_ref[:, lanes]
        for part in range(2):
            half = slice(part * COLS // 2, (part + 1) * COLS // 2)
            out[2 * COLS :, 2 * part * HID : (2 * part + 1) * HID] = self_ref[half]
            out[2 * COLS :, (2 * part + 1) * HID : (2 * part + 2) * HID] = neigh_ref[half]


def pack(x, up, self_weight, neigh_weight):
    return local_call(
        pack_kernel,
        [shape(EARLY, HALF)] * 2,
        [x, up, self_weight, neigh_weight],
        "pack",
        places={},
        flops=0,
        mib=60,
    )


GATHER_STEPS = 4


def gather_kernel(x_ref, slot_ref, hub_ref, out_hbm, out_ref, stacked, sems):
    for b in range(HIGH):
        stacked[b * COLS : (b + 1) * COLS, :] = x_ref[:, b * LOW : (b + 1) * LOW]
    group = DOM // GATHER_STEPS
    copies = []
    for step in range(GATHER_STEPS):
        for r in range(step * group, (step + 1) * group):
            index = slot_ref[r : r + 1, :]
            high = index >> 8
            found = dot(stacked[...], one_hot(index & (LOW - 1)), NN)
            out = jnp.zeros((COLS, SLOTS), F32)
            for b in range(HIGH):
                out = jnp.where(high == b, found[b * COLS : (b + 1) * COLS], out)
            out = out.astype(BF)
            out_ref[r, 0] = out[:, :TILE]
            out_ref[r, 1] = out[:, TILE:]
            out_ref[r, 2] = hub_ref[...]
        part = pl.ds(step * group, group)
        copies.append(pltpu.make_async_copy(out_ref.at[part], out_hbm.at[part], sems.at[step]))
        copies[step].start()
    for copy in copies:
        copy.wait()


def gather_rows(x, slots, hubs):
    return local_call(
        gather_kernel,
        [shape(DOM, 3, COLS, TILE)],
        [x, slots, hubs],
        "gather_rows",
        places={100: ANY},
        scratch=[
            pltpu.VMEM((DOM, 3, COLS, TILE), BF),
            pltpu.VMEM((HIGH * COLS, LOW), BF),
            pltpu.SemaphoreType.DMA((GATHER_STEPS,)),
        ],
        flops=4 * 10**9,
        mib=60,
    )[0]


def prepare_kernel(index_ref, x_ref, tile_hbm, list_hbm, sorted_hbm, total_hbm, list_ref, total_ref, tile_ref, sems):
    copy = pltpu.make_async_copy(tile_hbm, tile_ref, sems.at[0])
    copy.start()
    copy.wait()

    def sort(c, count):
        source = index_ref[1, c]
        own = source < OWN_TILES
        to = jnp.where(own, RECV_TILES + jnp.minimum(count, LOCAL_TILES - 1), source - OWN_TILES)
        list_ref[to] = index_ref[0, c]
        list_ref[TILES + to] = c
        pltpu.make_async_copy(tile_ref.at[c], sorted_hbm.at[to], sems.at[1]).start()
        return count + own.astype(I32)

    lax.fori_loop(0, TILES, sort, jnp.int32(0))
    total_ref[...] = jnp.zeros_like(total_ref)
    group = 8

    @pl.loop(0, LOCAL_TILES // group)
    def _(g):
        products = []
        for k in range(group):
            place = RECV_TILES + g * group + k
            c = list_ref[TILES + place]
            s = jnp.minimum(index_ref[1, c], OWN_TILES - 1)
            list_ref[TILES + place] = s
            lanes = pl.ds(pl.multiple_of(s * TILE, TILE), TILE)
            products.append(dot(tile_ref[c], x_ref[:, lanes], NT))
        for k in range(group):
            d = list_ref[RECV_TILES + g * group + k]
            total_ref[d] = total_ref[d] + products[k]

    outs = [
        pltpu.make_async_copy(total_ref, total_hbm.at[pl.ds(0, OWN_TILES)], sems.at[2]),
        pltpu.make_async_copy(list_ref, list_hbm.at[0], sems.at[3]),
    ]
    for copy in outs:
        copy.start()
    for copy in outs:
        copy.wait()
    pltpu.make_async_copy(tile_ref, sorted_hbm.at[pl.ds(0, TILES)], sems.at[1]).wait()


def prepare(index, x, tiles):
    return local_call(
        prepare_kernel,
        [
            shape(LISTS, LIST, dtype=I32),
            shape(SPARE_TILES, TILE, TILE),
            shape(SPARE_SUMS, TILE, COLS, dtype=F32),
        ],
        [index, x, tiles],
        "prepare",
        places={0: SMEM, 2: ANY, 100: ANY, 101: ANY, 102: ANY},
        scratch=[
            pltpu.SMEM((LIST,), I32),
            pltpu.VMEM((OWN_TILES, TILE, COLS), F32),
            pltpu.VMEM((TILES, TILE, TILE), BF),
            pltpu.SemaphoreType.DMA((4,)),
        ],
        mib=60,
    )


HUB_STEPS = 4
KEEP_EARLY = 1
TILE_STEPS = 4
HALF_ROWS = HALF // HUB_STEPS


def half_rows(half, step):
    return pl.ds(pl.multiple_of(half * HALF + step * HALF_ROWS, HALF_ROWS), HALF_ROWS)


def add_hub_rows(hub_ref, half, step, hubs, total, first_tile):
    tiles = HALF_ROWS // TILE
    part = dot(hub_ref[half_rows(half, step)], hubs[...], NT)
    for k in range(tiles):
        t = first_tile + step * tiles + k
        total[t] = total[t] + part[k * TILE : (k + 1) * TILE]


def forward_send_kernel(list_hbm, recv_ref, tile_hbm, local_hbm, hub_hbm, *rest):
    send_ref, keep_ref, hubs, hub_ref, target_ref, tile_ref, total, sems = rest
    away = 1 - chip()
    firsts = [
        pltpu.make_async_copy(src, dst, sems.at[2 * HUB_STEPS + i])
        for i, (src, dst) in enumerate(
            (
                (list_hbm.at[0], target_ref),
                (local_hbm.at[pl.ds(0, OWN_TILES)], total),
            )
        )
    ]
    group = RECV_TILES // TILE_STEPS
    tile_copies = []
    for i in range(TILE_STEPS):
        part = pl.ds(i * group, group)
        tile_copies.append(
            pltpu.make_async_copy(tile_hbm.at[part], tile_ref.at[part], sems.at[2 * HUB_STEPS + 2 + i])
        )
    copies = []
    for h, half in enumerate((away, chip())):
        for i in range(KEEP_EARLY if h else HUB_STEPS):
            rows = half_rows(half, i)
            copies.append(pltpu.make_async_copy(hub_hbm.at[rows], hub_ref.at[rows], sems.at[h * HUB_STEPS + i]))
    for copy in tile_copies[:1] + firsts + tile_copies[1:] + copies:
        copy.start()
    for q in range(DOM):
        hubs[:, q * TILE : (q + 1) * TILE] = recv_ref[q, 2]
    for step in range(TILE_STEPS):
        first = step * group
        tile_copies[step].wait()
        products = [dot(tile_ref[first + k], recv_ref[first // 2 + k // 2, k % 2], NT) for k in range(group)]
        if step == 0:
            for copy in firsts:
                copy.wait()
        for k, product in enumerate(products):
            d = target_ref[first + k]
            total[d] = total[d] + product

    for step in range(HUB_STEPS):
        copies[step].wait()
        add_hub_rows(hub_ref, away, step, hubs, total, away * HALF_TILES)
    for j in range(HALF_TILES):
        send_ref[:, j * TILE : (j + 1) * TILE] = total[away * HALF_TILES + j].T.astype(BF)
        keep_ref[j] = total[chip() * HALF_TILES + j]
    for copy in copies[HUB_STEPS:]:
        copy.wait()


def forward_send(lists, recv, tiles, local, hub_coef):
    return local_call(
        forward_send_kernel,
        [
            shape(COLS, HALF),
            shape(HALF_TILES, TILE, COLS, dtype=F32),
            shape(COLS, HUBS),
            shape(NODES, HUBS),
        ],
        [lists, recv, tiles, local, hub_coef],
        "forward_send",
        places={0: ANY, 2: ANY, 3: ANY, 4: ANY},
        scratch=[
            pltpu.SMEM((LIST,), I32),
            pltpu.VMEM((RECV_TILES, TILE, TILE), BF),
            pltpu.VMEM((OWN_TILES, TILE, COLS), F32),
            pltpu.SemaphoreType.DMA((2 * HUB_STEPS + 2 + TILE_STEPS,)),
        ],
        flops=2 * 10**9,
        size=2**24,
        mib=34,
    )


def forward_keep_kernel(sum_ref, hubs, _, hub_hbm, keep_ref, hub_ref, total, sems):
    copies = []
    for i in range(KEEP_EARLY, HUB_STEPS):
        rows = half_rows(chip(), i)
        copies.append(pltpu.make_async_copy(hub_hbm.at[rows], hub_ref.at[rows], sems.at[i]))
    for copy in copies:
        copy.start()
    total[...] = sum_ref[...]
    for step in range(HUB_STEPS):
        if step >= KEEP_EARLY:
            copies[step - KEEP_EARLY].wait()
        add_hub_rows(hub_ref, chip(), step, hubs, total, 0)
    for j in range(HALF_TILES):
        keep_ref[:, j * TILE : (j + 1) * TILE] = total[j].T.astype(BF)


def forward_keep(sums, hubs, hub, hub_coef):
    return local_call(
        forward_keep_kernel,
        [shape(COLS, HALF), shape(NODES, HUBS)],
        [sums, hubs, hub, hub_coef],
        "forward_keep",
        places={3: ANY},
        scratch=[pltpu.VMEM(sums.shape, F32), pltpu.SemaphoreType.DMA((HUB_STEPS,))],
        size=2**23,
        mib=28,
        alias={2: 1},
    )


def chip():
    return lax.axis_index("feat") // 2


def rows_of(k):
    return pl.ds(pl.multiple_of((lax.axis_index("feat") ^ k) * COLS, COLS), COLS)


def dense_kernel(*rest):
    aggs, earlies, outs, scratch = rest[:4], rest[4:8], rest[8:14], rest[14:]
    keep_grad, send_grad, grad_ref, self_ref, keep_out, send_out = outs
    agg, x, up, neigh_ref, output = scratch
    for k in range(FEAT):
        rows = rows_of(k)
        agg[rows] = aggs[k][...]
        x[rows] = earlies[k][:COLS]
        up[rows] = earlies[k][COLS : 2 * COLS]
        for part in range(2):
            packed = earlies[k][2 * COLS :, part * 2 * HID : (part + 1) * 2 * HID]
            first = (lax.axis_index("feat") ^ k) * COLS + part * COLS // 2
            half = pl.ds(pl.multiple_of(first, COLS // 2), COLS // 2)
            self_ref[half] = packed[:, :HID]
            neigh_ref[half] = packed[:, HID:]
    pre_act = dot(self_ref[...], x[...], TN) + dot(neigh_ref[...], agg[...], TN)
    fall = jnp.exp(jnp.minimum(pre_act, 0.0))
    output[...] = jnp.where(pre_act > 0, pre_act, fall - 1.0).astype(BF)
    slope = jnp.where(pre_act > 0, 1.0, fall)
    grad_pre = (up[...].astype(F32) * slope).astype(BF)
    grad_ref[...] = grad_pre
    weight = jnp.concatenate([neigh_ref[rows_of(0)], neigh_ref[rows_of(2)]], 0)
    grad_agg = dot(weight, grad_pre, NN).astype(BF)
    keep_grad[...] = grad_agg[:COLS]
    send_grad[...] = grad_agg[COLS:]
    keep_out[...] = output[rows_of(0)]
    send_out[...] = output[rows_of(2)]


def dense(aggs, earlies):
    block = pltpu.VMEM((HID, HALF), BF)
    return local_call(
        dense_kernel,
        [shape(COLS, HALF)] * 2 + [shape(HID, HALF), shape(HID, HID)] + [shape(COLS, HALF)] * 2,
        [*aggs, *earlies],
        "dense",
        places={},
        scratch=[block] * 3 + [pltpu.VMEM((HID, HID), BF), block],
    )


HUB_LANES = HUBS // HUB_STEPS


def hub_part(half, step):
    return pl.ds(pl.multiple_of(half * HALF, HALF), HALF), slice(step * HUB_LANES, (step + 1) * HUB_LANES)


def hub_backward_kernel(grad_ref, self_ref, pre_ref, hub_ref, out_ref, keep_back, send_back):
    weight = jnp.concatenate([self_ref[rows_of(0)], self_ref[rows_of(2)]], 0)
    back = dot(weight, pre_ref[...], NN).astype(BF)
    keep_back[...] = back[:COLS]
    send_back[...] = back[COLS:]
    for step in range(HUB_STEPS):
        rows, lanes = hub_part(chip(), step)
        out_ref[:, lanes] = dot(grad_ref[...], hub_ref[rows, lanes], NN)


def hub_backward(grad, self_weight, grad_pre, hub):
    return local_call(
        hub_backward_kernel,
        [shape(COLS, HUBS, dtype=F32), shape(COLS, HALF), shape(COLS, HALF)],
        [grad, self_weight, grad_pre, hub],
        "hub_backward",
        places={},
        size=2**23,
        mib=20,
    )


def split_tiles(keep_ref, come_ref, grads):
    for k, part in enumerate((keep_ref, come_ref)):
        first = (chip() ^ k) * HALF_TILES
        for j in range(HALF_TILES):
            grads[first + j] = part[:, j * TILE : (j + 1) * TILE]


def backward_kernel(list_hbm, keep_ref, come_ref, terms_ref, tile_hbm, hub_ref, *rest):
    out_hbm, out_ref, target_ref, grads, tile_ref, sems = rest
    group = RECV_TILES // HUB_STEPS
    doms = DOM // HUB_STEPS
    out_copies = []
    list_copy = pltpu.make_async_copy(list_hbm.at[0], target_ref, sems.at[HUB_STEPS])
    list_copy.start()
    copies = []
    for i in range(HUB_STEPS):
        part = pl.ds(i * group, group)
        copies.append(pltpu.make_async_copy(tile_hbm.at[part], tile_ref.at[part], sems.at[i]))
        copies[i].start()
    split_tiles(keep_ref, come_ref, grads)
    list_copy.wait()
    for step in range(HUB_STEPS):
        rows, lanes = hub_part(1 - chip(), step)
        terms = (terms_ref[:, lanes] + dot(come_ref[...], hub_ref[rows, lanes], NN)).astype(BF)
        for k in range(doms):
            out_ref[step * doms + k, 2] = terms[:, k * TILE : (k + 1) * TILE]
        copies[step].wait()
        for s in range(step * group, (step + 1) * group):
            out_ref[s // 2, s % 2] = dot(grads[target_ref[s]], tile_ref[s], NN).astype(BF)
        part = pl.ds(step * doms, doms)
        out_copies.append(pltpu.make_async_copy(out_ref.at[part], out_hbm.at[part], sems.at[HUB_STEPS + 1 + step]))
        out_copies[step].start()
    for copy in out_copies:
        copy.wait()


def backward(lists, keep, come, terms, tiles, hub):
    return local_call(
        backward_kernel,
        [shape(DOM, 3, COLS, TILE)],
        [lists, keep, come, terms, tiles, hub],
        "backward",
        places={0: ANY, 4: ANY, 100: ANY},
        scratch=[
            pltpu.VMEM((DOM, 3, COLS, TILE), BF),
            pltpu.SMEM((LIST,), I32),
            pltpu.VMEM((OWN_TILES, COLS, TILE), BF),
            pltpu.VMEM((RECV_TILES, TILE, TILE), BF),
            pltpu.SemaphoreType.DMA((2 * HUB_STEPS + 1,)),
        ],
        flops=2 * 10**9,
        size=2**23,
        mib=20,
    )[0]


def own_backward_kernel(list_hbm, keep_ref, come_ref, tile_hbm, own_hbm, *rest):
    list_ref, own_ref, grads, total, tile_ref, sems = rest
    copies = [
        pltpu.make_async_copy(list_hbm.at[0], list_ref, sems.at[0]),
        pltpu.make_async_copy(tile_hbm.at[pl.ds(RECV_TILES, LOCAL_TILES)], tile_ref, sems.at[1]),
    ]
    for copy in copies:
        copy.start()
    split_tiles(keep_ref, come_ref, grads)
    total[...] = jnp.zeros_like(total)
    for copy in copies:
        copy.wait()
    group = 8

    @pl.loop(0, LOCAL_TILES // group)
    def _(g):
        places = [RECV_TILES + g * group + k for k in range(group)]
        products = [dot(grads[list_ref[c]], tile_ref[c - RECV_TILES], NN) for c in places]
        for c, product in zip(places, products):
            s = list_ref[TILES + c]
            total[s] = total[s] + product

    for t in range(OWN_TILES):
        own_ref[:, t * TILE : (t + 1) * TILE] = total[t]
    out_copy = pltpu.make_async_copy(own_ref, own_hbm.at[pl.ds(0, COLS)], sems.at[2])
    out_copy.start()
    out_copy.wait()


def own_backward(lists, keep, come, tiles):
    return local_call(
        own_backward_kernel,
        [shape(SPARE_ROWS, NODES, dtype=F32)],
        [lists, keep, come, tiles],
        "own_backward",
        places={0: ANY, 3: ANY, 100: ANY},
        scratch=[
            pltpu.SMEM((LIST,), I32),
            pltpu.VMEM((COLS, NODES), F32),
            pltpu.VMEM((OWN_TILES, COLS, TILE), BF),
            pltpu.VMEM((OWN_TILES, COLS, TILE), F32),
            pltpu.VMEM((LOCAL_TILES, TILE, TILE), BF),
            pltpu.SemaphoreType.DMA((3,)),
        ],
        mib=60,
    )[0]


def scatter_kernel(slot_ref, recv_ref, own_hbm, keep_ref, come_ref, out_keep, out_come, *rest):
    grad_ref, hub_ref, output_ref, total, own_ref, sems = rest
    own_copy = pltpu.make_async_copy(own_hbm.at[pl.ds(0, COLS)], own_ref, sems.at[0])
    own_copy.start()
    total[...] = jnp.zeros_like(total)
    group = 16

    @pl.loop(0, DOM // group)
    def _(g):
        spread, hots = [], []
        for k in range(group):
            r = g * group + k
            index = slot_ref[pl.ds(r, 1), :]
            high = index >> 8
            rows = jnp.concatenate([recv_ref[r, 0], recv_ref[r, 1]], 1)
            spread.append(
                jnp.concatenate([jnp.where(high == b, rows, jnp.zeros_like(rows)) for b in range(HIGH)], 0)
            )
            hots.append(one_hot(index & (LOW - 1)))
        total[...] += dot(jnp.concatenate(spread, 1), jnp.concatenate(hots, 1), NT)

    hub = jnp.zeros((COLS, TILE), F32)
    for r in range(DOM):
        hub = hub + recv_ref[r, 2].astype(F32)
    hub_ref[...] = hub
    own_copy.wait()
    for b in range(HIGH):
        lanes = slice(b * LOW, (b + 1) * LOW)
        grad_ref[:, lanes] = total[b * COLS : (b + 1) * COLS] + own_ref[:, lanes]
    keep = pl.ds(pl.multiple_of(chip() * HALF, HALF), HALF)
    come = pl.ds(pl.multiple_of((1 - chip()) * HALF, HALF), HALF)
    grad_ref[:, keep] = grad_ref[:, keep] + keep_ref[...].astype(F32)
    grad_ref[:, come] = grad_ref[:, come] + come_ref[...].astype(F32)
    output_ref[:, keep] = out_keep[...]
    output_ref[:, come] = out_come[...]


def scatter_rows(slots, recv, own, keep, come, out_keep, out_come):
    return local_call(
        scatter_kernel,
        [shape(COLS, NODES, dtype=F32), shape(COLS, TILE, dtype=F32), shape(COLS, NODES)],
        [slots, recv, own, keep, come, out_keep, out_come],
        "scatter_rows",
        places={2: ANY},
        scratch=[
            pltpu.VMEM((HIGH * COLS, LOW), F32),
            pltpu.VMEM((COLS, NODES), F32),
            pltpu.SemaphoreType.DMA((1,)),
        ],
        mib=47,
    )


def to_dom(x):
    return lax.all_to_all(x, "dom", split_axis=0, concat_axis=0, tiled=True)


def swap(x, k):
    return lax.ppermute(x, "feat", [(f, f ^ k) for f in range(FEAT)])


def after(x, *others):
    return lax.optimization_barrier((x, *others))[0]


def body(
    features,
    hub_feats,
    hub_coef,
    tile_coef,
    tile_index,
    boundary_rows,
    self_weight,
    neigh_weight,
    out_grad,
):
    x = features.T
    up = out_grad.T
    slots = boundary_rows[0]
    index = tile_index.T

    outgoing = gather_rows(x, slots, hub_feats.T)
    incoming = to_dom(outgoing)
    x_in, up_in = lax.optimization_barrier((x, up, outgoing))[:2]
    early, early_send = pack(x_in, up_in, self_weight, neigh_weight)
    early_2 = swap(early_send, 2)
    early_1 = swap(early, 1)
    lists, tiles, local_sum = prepare(index, x_in, tile_coef)
    agg_send, sums, hubs, hub = forward_send(lists, incoming, tiles, local_sum, hub_coef)
    agg_2 = swap(agg_send, 2)
    agg, hub = forward_keep(sums, hubs, hub, hub_coef)
    early_2, agg_2, agg = lax.optimization_barrier((early_2, agg_2, agg))
    early = [early, early_1, early_2, swap(early_2, 1)]
    grad, grad_send, grad_pre, self_weight, out_keep, out_send = dense(
        [agg, swap(agg, 1), agg_2, swap(agg_2, 1)], early
    )
    grad_2 = swap(grad_send, 2)
    terms, back, back_send = hub_backward(grad, self_weight, grad_pre, hub)
    back_2 = swap(back_send, 2)
    sums = backward(lists, grad, grad_2, terms, tiles, hub)
    sums, back_2, out_send = lax.optimization_barrier((sums, back_2, out_send))
    returned = to_dom(sums)
    out_2 = swap(out_send, 2)
    own_grad = own_backward(lists, after(grad, sums), grad_2, tiles)
    grad_feats, grad_hubs, output_rows = scatter_rows(
        slots, returned, own_grad, back, back_2, out_keep, out_2
    )
    return (output_rows.T, grad_feats.T, grad_hubs.T)


def solution(mesh):
    return jax.shard_map(
        body,
        mesh=mesh,
        in_specs=(
            P("dom", "feat"),
            P("dom", "feat"),
            P("dom", None),
            P("dom", None, None),
            P("dom", None),
            P("dom", None, None),
            P("feat", None),
            P("feat", None),
            P("dom", "feat"),
        ),
        out_specs=(P("dom", "feat"), P("dom", "feat"), P("dom", "feat")),
        check_vma=False,
    )
```
